32 devices in a mesh: space: 8 (over y, x, core), chan: 4 (over z).
Axes of the slice: x: 2, y: 2, z: 4, core: 2. Of those that a mesh axis runs over, the one named last changes fastest.
Arguments:
- inputs: bfloat16 [128, 32, 32, 128], P('chan', 'space'), may hold values from -6 to 6
- filters: bfloat16 [27, 128, 128], P(None, 'chan'), may hold values from -0.109375 to 0.109375
- cotangent: bfloat16 [128, 32, 32, 128], P('chan', 'space'), may hold values from -6 to 6
Outputs:
- grad_inputs: bfloat16 [128, 32, 32, 128], P('chan', 'space')
- grad_filters: float32 [27, 128, 128], P(None, 'chan')
The draws below stay inside these ranges and needn't reach their ends.
All inputs are finite; a program needn't handle non-finite values.
Results may differ from the reference program's by a relative error of at most 0.0049.
Values may be sent and summed in bfloat16 or wider, within the bound.
No kernel may reach another device: no remote copies, remote signals or barrier semaphores. Data moves between devices by JAX's collectives and lax.ppermute only.
A program may use at most 128 MiB of HBM per device.

```python
import math
import jax
import jax.numpy as jnp

C = 128
HEIGHT = 32
WIDTH = 128
DEPTH = 32
CELLS = 131072


def level_of(rng, shape, shards, least, top_value):
    gain, own = 1.0, jax.random.fold_in(rng, 6)
    for dim, parts in shards:
        draws = jnp.exp(jax.random.uniform(jax.random.fold_in(own, dim), (parts,), jnp.float32, least / len(shards), top_value / len(shards)))
        gain = gain * jnp.repeat(draws, shape[dim] // parts).reshape([-1 if axis == dim else 1 for axis in range(len(shape))])
    return gain


def bell_draw(own_key, dims, scale, bound, shards=(), held_as=jnp.bfloat16):
    result = scale * jax.random.normal(own_key, dims, jnp.float32)
    if shards:
        result = result * level_of(own_key, dims, shards, -0.22, 0.18)
    return jnp.clip(result, -bound, bound).astype(held_as)


def setup_inputs(seed: int = 0) -> dict:
    arg_keys = jax.random.split(jax.random.key(seed), 4)
    inputs = bell_draw(arg_keys[0], (C, DEPTH, HEIGHT, WIDTH), 1.0, 6.0, ((0, 4), (1, 8)))
    filters = bell_draw(arg_keys[1], (27, C, C), (27 * C) ** -0.5, 0.109375, ((1, 4),))
    cotangent = bell_draw(arg_keys[2], (C, DEPTH, HEIGHT, WIDTH), 1.0, 6.0, ((0, 4), (1, 8)))
    return dict(inputs=inputs, filters=filters, cotangent=cotangent)


def reference(inputs, filters, cotangent):
    plane_count = inputs.shape[1]
    row_count = inputs.shape[2]
    column_count = inputs.shape[3]
    padded_in = jnp.pad(inputs.astype(jnp.float32), ((0, 0), (1, 1), (1, 1), (1, 1)))
    weights32 = filters.astype(jnp.float32)
    pre_act = jnp.zeros((C, plane_count, row_count, column_count), jnp.float32)
    for offset in range(27):
        depth_off = offset // 9
        row_off = offset // 3 % 3
        column_off = offset % 3
        window = padded_in[:, depth_off:depth_off + plane_count, row_off:row_off + row_count, column_off:column_off + column_count]
        pre_act = pre_act + jnp.einsum('io,idhw->odhw', weights32[offset], window)
    sigma = jax.nn.sigmoid(pre_act)
    grad_out = (cotangent.astype(jnp.float32) * sigma * (1.0 + pre_act * (1.0 - sigma))).astype(jnp.bfloat16)
    grad32 = grad_out.astype(jnp.float32)
    grad_pad = jnp.pad(grad32, ((0, 0), (1, 1), (1, 1), (1, 1)))
    grad_in = jnp.zeros((C, plane_count, row_count, column_count), jnp.float32)
    pieces = []
    for offset in range(27):
        depth_off = offset // 9
        row_off = offset // 3 % 3
        column_off = offset % 3
        window = grad_pad[:, 2 - depth_off:2 - depth_off + plane_count, 2 - row_off:2 - row_off + row_count, 2 - column_off:2 - column_off + column_count]
        grad_in = grad_in + jnp.einsum('io,odhw->idhw', weights32[offset], window)
        source = padded_in[:, depth_off:depth_off + plane_count, row_off:row_off + row_count, column_off:column_off + column_count]
        pieces.append(jnp.einsum('idhw,odhw->io', source, grad32))
    grad_w = jnp.stack(pieces) * (1.0 / math.sqrt(CELLS))
    return (grad_in.astype(jnp.bfloat16), grad_w)
```

```python
import functools
import math

import jax
import jax.numpy as jnp
from jax import lax
from jax.experimental import pallas as pl
from jax.experimental.pallas import tpu as pltpu
from jax.sharding import PartitionSpec as P

BF16 = jnp.bfloat16
F32 = jnp.float32
VMEM_BYTES = 56 * 1024 * 1024


def ring(count, step):
    return [(i, (i + step) % count) for i in range(count)]


def shift_sum(parts, groups, cells, up_first):
    first, mid, last = (p.reshape(groups, cells, -1) for p in parts)
    if up_first:
        first, last = last, first
    col = lax.broadcasted_iota(jnp.int32, mid.shape, 1)
    before = jnp.where(col == 0, 0.0, pltpu.roll(first, 1, 1))
    after = jnp.where(col == cells - 1, 0.0, pltpu.roll(last, cells - 1, 1))
    return mid + before + after


def forward_kernel(chan_count, z_ref, *refs):
    pieces = refs[:chan_count]
    low_ref, high_ref, weights_ref, slope_ref, first_ref, last_ref = refs[chan_count:]
    rows, planes, group, cells = pieces[0].shape
    channels = group * chan_count
    z = z_ref[0]
    offsets = [
        pl.multiple_of(lax.rem(z - j + chan_count, chan_count) * group, group)
        for j in range(chan_count)
    ]

    @pl.loop(0, rows)
    def _(r):
        for j in range(chan_count):
            for p in range(planes):
                first_ref[r, p + 1, pl.ds(offsets[j], group), :] = pieces[j][r, p]
            first_ref[r, 0, pl.ds(offsets[j], group), :] = low_ref[
                r, 0, j * group : (j + 1) * group, :
            ]
            first_ref[r, planes + 1, pl.ds(offsets[j], group), :] = high_ref[
                r, 0, j * group : (j + 1) * group, :
            ]
        for p in range(planes + 2):
            last_ref[r, p] = first_ref[r, p].T

    @pl.loop(0, rows - 2)
    def _(r):
        lhs = jnp.concatenate(
            [
                last_ref[r + b, a : a + planes].reshape(planes * cells, channels)
                for a in range(3)
                for b in range(3)
            ],
            axis=1,
        )
        out = jnp.dot(lhs, weights_ref[...], preferred_element_type=F32)
        pre = shift_sum(
            [out[:, c * channels : (c + 1) * channels] for c in range(3)], planes, cells, False
        )
        sigma = 1.0 / (1.0 + jnp.exp(-pre))
        slope_ref[r] = sigma * (1.0 + pre * (1.0 - sigma))


def grad_out_kernel(chan_count, z_ref, *refs):
    pieces = refs[:chan_count]
    slope_ref, grad_ref, low_ref, high_ref, hold_ref = refs[chan_count:]
    rows, planes, group, cells = pieces[0].shape
    z = z_ref[0]
    offsets = [
        pl.multiple_of(lax.rem(z - j + chan_count, chan_count) * group, group)
        for j in range(chan_count)
    ]

    @pl.loop(0, rows)
    def _(r):
        for p in range(planes):
            for j in range(chan_count):
                hold_ref[p, pl.ds(offsets[j], group), :] = pieces[j][r, p]
        for p in range(planes):
            cot = hold_ref[p].T.astype(F32)
            grad = (cot * slope_ref[r, p]).astype(BF16)
            grad_ref[r, p] = grad
            if p == 0:
                low_ref[r] = grad
            if p == planes - 1:
                high_ref[r] = grad


def filter_kernel(chan_count, space_count, shard, core_ref, x_ref, grad_ref, keep_ref, send_ref, acc_ref, pack_ref):
    rows = grad_ref.shape[0] - 2
    planes, cells, channels = grad_ref.shape[1:]
    group = channels // chan_count
    acc_ref[...] = jnp.zeros_like(acc_ref)

    @pl.loop(0, rows)
    def _(h):
        lhs = jnp.concatenate(
            [
                jnp.concatenate([x_ref[h + 1 + b, d + a] for d in range(planes)], axis=1)
                for a in range(3)
                for b in range(3)
            ],
            axis=0,
        )
        grad = grad_ref[h + 1].astype(F32)
        col = lax.broadcasted_iota(jnp.int32, grad.shape, 1)
        after = jnp.where(col == cells - 1, 0.0, pltpu.roll(grad, cells - 1, 1))
        before = jnp.where(col == 0, 0.0, pltpu.roll(grad, 1, 1))
        rhs = jnp.concatenate(
            [v.astype(BF16).reshape(planes * cells, channels) for v in (after, grad, before)],
            axis=1,
        )
        acc_ref[...] += jnp.dot(lhs, rhs, preferred_element_type=F32)

    used = 27 * group
    for z in range(chan_count):
        for offset in range(27):
            row = (offset // 3) * channels + z * group
            col = (offset % 3) * channels
            pack_ref[z, offset * group : (offset + 1) * group, :] = acc_ref[
                row : row + group, col : col + channels
            ]
        pack_ref[z, used:, :] = jnp.zeros((space_count * shard - used, channels), F32)
    core = core_ref[0]
    for chip in range(space_count // 2):
        mine = pl.multiple_of((2 * chip + core) * shard, 8)
        other = pl.multiple_of((2 * chip + 1 - core) * shard, 8)
        for z in range(chan_count):
            keep_ref[chip, z] = pack_ref[z, pl.ds(mine, shard), :]
            send_ref[chip, z] = pack_ref[z, pl.ds(other, shard), :]


def input_kernel(chan_count, z_ref, grad_ref, low_ref, high_ref, weights_ref, *refs):
    outs = refs[:chan_count]
    hold_ref = refs[chan_count]
    rows = grad_ref.shape[0] - 2
    planes, cells, channels = grad_ref.shape[1:]
    group = channels // chan_count
    z = z_ref[0]
    offsets = [
        pl.multiple_of(lax.rem(z + j, chan_count) * group, group) for j in range(chan_count)
    ]

    @pl.loop(0, rows)
    def _(h):
        columns = []
        for a in range(3):
            for b in range(3):
                r = h + 2 - b
                if a == 1:
                    columns.append(grad_ref[r].reshape(planes * cells, channels))
                elif a == 0:
                    body = grad_ref[r, 1:planes].reshape((planes - 1) * cells, channels)
                    columns.append(jnp.concatenate([body, high_ref[r]], axis=0))
                else:
                    body = grad_ref[r, 0 : planes - 1].reshape((planes - 1) * cells, channels)
                    columns.append(jnp.concatenate([low_ref[r], body], axis=0))
        out = jnp.dot(
            jnp.concatenate(columns, axis=1), weights_ref[...], preferred_element_type=F32
        )
        total = shift_sum(
            [out[:, c * channels : (c + 1) * channels] for c in range(3)], planes, cells, True
        ).astype(BF16)
        for p in range(planes):
            hold_ref[p] = total[p].T
        for j in range(chan_count):
            for p in range(planes):
                outs[j][h, p] = hold_ref[p, pl.ds(offsets[j], group), :]


def call(kernel, outs, scratch, flops, args, scalar):
    nbytes = sum(math.prod(a.shape) * a.dtype.itemsize for a in list(args) + list(outs))
    return pl.pallas_call(
        kernel,
        out_shape=outs,
        in_specs=[pl.BlockSpec(memory_space=pltpu.SMEM)]
        + [pl.BlockSpec(memory_space=pltpu.VMEM)] * len(args),
        out_specs=[pl.BlockSpec(memory_space=pltpu.VMEM)] * len(outs),
        scratch_shapes=scratch,
        compiler_params=pltpu.CompilerParams(vmem_limit_bytes=VMEM_BYTES),
        cost_estimate=pl.CostEstimate(flops=flops, bytes_accessed=nbytes, transcendentals=0),
    )(scalar, *args)


def row_blocks(array, halo, z, chan_count):
    turned = jnp.pad(array.transpose(2, 1, 0, 3), ((halo, halo), (0, 0), (0, 0), (0, 0)))
    rows = array.shape[2] // chan_count
    return [
        lax.dynamic_slice_in_dim(turned, lax.rem(z + j, chan_count) * rows, rows + 2 * halo, axis=0)
        for j in range(chan_count)
    ]


def exchange(blocks, axis):
    count = len(blocks)
    return [blocks[0]] + [
        lax.ppermute(blocks[j], axis, ring(count, j)) for j in range(1, count)
    ]


def body(inputs, filters, cotangent):
    chan_count = lax.axis_size("chan")
    space_count = lax.axis_size("space")
    group, planes, height, cells = inputs.shape
    channels = group * chan_count
    rows = height // chan_count
    z = lax.axis_index("chan").astype(jnp.int32)
    s = lax.axis_index("space").astype(jnp.int32)
    upward = [(i, i + 1) for i in range(space_count - 1)]
    downward = [(i + 1, i) for i in range(space_count - 1)]
    shape = jax.ShapeDtypeStruct
    z_arg = z.reshape(1)

    x_pieces = exchange(row_blocks(inputs, 2, z, chan_count), "chan")
    filter_all = lax.all_gather(filters, "chan", axis=1, tiled=True)
    by_offset = filter_all.reshape(9, 3, channels, channels)
    weights_f = by_offset.transpose(0, 2, 1, 3).reshape(9 * channels, 3 * channels)
    weights_b = by_offset.transpose(0, 3, 1, 2).reshape(9 * channels, 3 * channels)

    x_top = jnp.concatenate([p[:, planes - 1 :] for p in x_pieces], axis=2)
    x_bottom = jnp.concatenate([p[:, :1] for p in x_pieces], axis=2)
    x_low = lax.ppermute(x_top, "space", upward)
    x_high = lax.ppermute(x_bottom, "space", downward)
    c_pieces = exchange(row_blocks(cotangent, 1, z, chan_count), "chan")

    macs = 27 * channels * channels * rows * planes * cells
    padded = (rows + 4, planes + 2, channels, cells)
    slope, x_first = call(
        functools.partial(forward_kernel, chan_count),
        [shape((rows + 2, planes, cells, channels), F32), shape(padded, BF16)],
        [pltpu.VMEM((rows + 4, planes + 2, cells, channels), BF16)],
        2 * macs * (rows + 2) // rows,
        [*x_pieces, x_low, x_high, weights_f],
        z_arg,
    )
    grad, g_bottom, g_top = call(
        functools.partial(grad_out_kernel, chan_count),
        [shape((rows + 2, planes, cells, channels), BF16)]
        + [shape((rows + 2, cells, channels), BF16)] * 2,
        [pltpu.VMEM((planes, channels, cells), BF16)],
        10 * rows * planes * cells * channels,
        [*c_pieces, slope],
        z_arg,
    )
    g_low = lax.ppermute(g_top, "space", upward)
    g_high = lax.ppermute(g_bottom, "space", downward)

    chips = space_count // 2
    shard = -(-27 * group // (16 * space_count)) * 16
    half = shape((chips, chan_count, shard, channels), F32)
    keep, send = call(
        functools.partial(filter_kernel, chan_count, space_count, shard),
        [half, half],
        [
            pltpu.VMEM((9 * channels, 3 * channels), F32),
            pltpu.VMEM((chan_count, space_count * shard, channels), F32),
        ],
        2 * macs,
        [x_first, grad],
        lax.rem(s, 2).reshape(1),
    )
    from_core = lax.ppermute(send, "space", [(i, i ^ 1) for i in range(space_count)])

    back = call(
        functools.partial(input_kernel, chan_count),
        [shape((rows, planes, group, cells), BF16)] * chan_count,
        [pltpu.VMEM((planes, channels, cells), BF16)],
        2 * macs,
        [grad, g_low, g_high, weights_b],
        z_arg,
    )
    returned = exchange(back, "chan")

    pair_sum = keep + from_core
    chip = s // 2
    own = lax.dynamic_index_in_dim(pair_sum, chip, 0, keepdims=False)
    rounded = pair_sum.astype(BF16)
    chip_sum = own
    for k in range(1, chips):
        block = lax.dynamic_index_in_dim(rounded, chip ^ k, 0, keepdims=False)
        got = lax.ppermute(block, "space", [(i, i ^ (2 * k)) for i in range(space_count)])
        chip_sum = chip_sum + got.astype(F32)
    parts = [
        lax.dynamic_index_in_dim(chip_sum, lax.rem(z + j, chan_count), 0, keepdims=False)
        for j in range(chan_count)
    ]
    shard_sum = sum(exchange(parts, "chan"))
    cell_total = planes * space_count * height * cells
    shard_sum = shard_sum * (1.0 / math.sqrt(cell_total))
    whole = lax.all_gather(shard_sum, "space", axis=0, tiled=True)
    grad_w = whole[: 27 * group].reshape(27, group, channels)

    reverse = returned[::-1]
    doubled = jnp.concatenate(reverse + reverse, axis=0)
    start = lax.rem(chan_count - 1 - z + chan_count, chan_count) * rows
    ordered = lax.dynamic_slice_in_dim(doubled, start, height, axis=0)
    return ordered.transpose(2, 1, 0, 3), grad_w


def solution(mesh):
    placed = (P("chan", "space", None, None), P(None, "chan", None), P("chan", "space", None, None))
    return jax.shard_map(
        body,
        mesh=mesh,
        in_specs=placed,
        out_specs=(P("chan", "space", None, None), P(None, "chan", None)),
        check_vma=False,
    )
```

```python
import functools
import math

import jax
import jax.numpy as jnp
from jax import lax
from jax.experimental import pallas as pl
from jax.experimental.pallas import tpu as pltpu
from jax.sharding import PartitionSpec as P

BF16 = jnp.bfloat16
F32 = jnp.float32
VMEM_BYTES = 56 * 1024 * 1024


def ring(count, step):
    return [(i, (i + step) % count) for i in range(count)]


def shift_sum(parts, groups, cells, up_first):
    first, mid, last = (p.reshape(groups, cells, -1) for p in parts)
    if up_first:
        first, last = last, first
    col = lax.broadcasted_iota(jnp.int32, mid.shape, 1)
    before = jnp.where(col == 0, 0.0, pltpu.roll(first, 1, 1))
    after = jnp.where(col == cells - 1, 0.0, pltpu.roll(last, cells - 1, 1))
    return mid + before + after


def kept(flag, value):
    return jnp.where(flag > 0, value, jnp.zeros_like(value))


def forward_kernel(chan_count, z_ref, *refs):
    pieces = refs[:chan_count]
    low_ref, high_ref, weights_ref, slope_ref, first_ref, last_ref = refs[chan_count:]
    rows, planes, group, cells = pieces[0].shape
    channels = group * chan_count
    z = z_ref[0]
    offsets = [
        pl.multiple_of(lax.rem(z - j + chan_count, chan_count) * group, group)
        for j in range(chan_count)
    ]

    @pl.loop(0, rows)
    def _(r):
        for j in range(chan_count):
            for p in range(planes):
                first_ref[r, p + 1, pl.ds(offsets[j], group), :] = pieces[j][r, p]
            part = slice(j * group, (j + 1) * group)
            first_ref[r, 0, pl.ds(offsets[j], group), :] = kept(z_ref[1], low_ref[r, 0, part, :])
            first_ref[r, planes + 1, pl.ds(offsets[j], group), :] = kept(
                z_ref[2], high_ref[r, 0, part, :]
            )
        for p in range(planes + 2):
            last_ref[r, p] = first_ref[r, p].T

    @pl.loop(0, rows - 2)
    def _(r):
        lhs = jnp.concatenate(
            [
                last_ref[r + b, a : a + planes].reshape(planes * cells, channels)
                for a in range(3)
                for b in range(3)
            ],
            axis=1,
        )
        out = jnp.dot(lhs, weights_ref[...], preferred_element_type=F32)
        pre = shift_sum(
            [out[:, c * channels : (c + 1) * channels] for c in range(3)], planes, cells, False
        )
        sigma = 1.0 / (1.0 + jnp.exp(-pre))
        slope_ref[r] = sigma * (1.0 + pre * (1.0 - sigma))


def grad_out_kernel(chan_count, z_ref, *refs):
    pieces = refs[:chan_count]
    slope_ref, grad_ref, low_ref, high_ref, hold_ref = refs[chan_count:]
    rows, planes, group, cells = pieces[0].shape
    z = z_ref[0]
    offsets = [
        pl.multiple_of(lax.rem(z - j + chan_count, chan_count) * group, group)
        for j in range(chan_count)
    ]

    @pl.loop(0, rows)
    def _(r):
        for p in range(planes):
            for j in range(chan_count):
                hold_ref[p, pl.ds(offsets[j], group), :] = pieces[j][r, p]
        for p in range(planes):
            cot = hold_ref[p].T.astype(F32)
            grad = (cot * slope_ref[r, p]).astype(BF16)
            grad_ref[r, p] = grad
            if p == 0:
                low_ref[r] = grad
            if p == planes - 1:
                high_ref[r] = grad


def filter_kernel(
    chan_count, space_count, shard, core_ref, x_ref, grad_ref, keep_ref, send_ref, acc_ref, pack_ref
):
    rows, planes, cells, channels = grad_ref.shape
    group = channels // chan_count
    acc_ref[...] = jnp.zeros_like(acc_ref)

    @pl.loop(0, rows)
    def _(h):
        lhs = jnp.concatenate(
            [
                jnp.concatenate([x_ref[h + b, d + a] for d in range(planes)], axis=1)
                for a in range(3)
                for b in range(3)
            ],
            axis=0,
        )
        grad = grad_ref[h].astype(F32)
        col = lax.broadcasted_iota(jnp.int32, grad.shape, 1)
        after = jnp.where(col == cells - 1, 0.0, pltpu.roll(grad, cells - 1, 1))
        before = jnp.where(col == 0, 0.0, pltpu.roll(grad, 1, 1))
        rhs = jnp.concatenate(
            [v.astype(BF16).reshape(planes * cells, channels) for v in (after, grad, before)],
            axis=1,
        )
        acc_ref[...] += jnp.dot(lhs, rhs, preferred_element_type=F32)

    used = 27 * group
    for z in range(chan_count):
        for offset in range(27):
            row = (offset // 3) * channels + z * group
            col = (offset % 3) * channels
            pack_ref[z, offset * group : (offset + 1) * group, :] = acc_ref[
                row : row + group, col : col + channels
            ]
        pack_ref[z, used:, :] = jnp.zeros((space_count * shard - used, channels), F32)
    core = core_ref[0]
    for chip in range(space_count // 2):
        mine = pl.multiple_of((2 * chip + core) * shard, 8)
        other = pl.multiple_of((2 * chip + 1 - core) * shard, 8)
        for z in range(chan_count):
            keep_ref[chip, z] = pack_ref[z, pl.ds(mine, shard), :]
            send_ref[chip, z] = pack_ref[z, pl.ds(other, shard), :]


def input_row(center, low, high, weights_ref, hold_ref, offsets):
    columns = []
    planes, cells, channels = center(1).shape
    for a in range(3):
        for b in range(3):
            row = center(b)
            if a == 1:
                part = row.reshape(planes * cells, channels)
            elif a == 0:
                body = row[1:].reshape((planes - 1) * cells, channels)
                part = jnp.concatenate([body, high(b)], axis=0)
            else:
                body = row[: planes - 1].reshape((planes - 1) * cells, channels)
                part = jnp.concatenate([low(b), body], axis=0)
            columns.append(part)
    out = jnp.dot(jnp.concatenate(columns, axis=1), weights_ref[...], preferred_element_type=F32)
    total = shift_sum(
        [out[:, c * channels : (c + 1) * channels] for c in range(3)], planes, cells, True
    ).astype(BF16)
    for p in range(planes):
        hold_ref[p] = total[p].T
    group = channels // len(offsets)
    return [
        jnp.stack([hold_ref[p, pl.ds(offset, group), :] for p in range(planes)])
        for offset in offsets
    ]


def group_offsets(z, chan_count, group):
    return [pl.multiple_of(lax.rem(z + j, chan_count) * group, group) for j in range(chan_count)]


def inner_kernel(chan_count, z_ref, grad_ref, low_ref, high_ref, weights_ref, *refs):
    outs, hold_ref = refs[:chan_count], refs[chan_count]
    rows, planes, cells, channels = grad_ref.shape
    offsets = group_offsets(z_ref[0], chan_count, channels // chan_count)

    @pl.loop(1, rows - 1)
    def _(h):
        blocks = input_row(
            lambda b: grad_ref[h + 1 - b],
            lambda b: kept(z_ref[1], low_ref[h + 1 - b]),
            lambda b: kept(z_ref[2], high_ref[h + 1 - b]),
            weights_ref,
            hold_ref,
            offsets,
        )
        for out, block in zip(outs, blocks):
            out[h - 1] = block


def edge_kernel(chan_count, z_ref, grad_ref, low_ref, high_ref, up_ref, down_ref, weights_ref, *refs):
    inner, outs, hold_ref = refs[:chan_count], refs[chan_count : 2 * chan_count], refs[-1]
    rows, planes, cells, channels = grad_ref.shape
    offsets = group_offsets(z_ref[0], chan_count, channels // chan_count)
    for j in range(chan_count):
        outs[j][1 : rows - 1] = inner[j][...]

    def pick(h, b, beyond, inside):
        row = h + 1 - b
        if row < 0:
            return kept(z_ref[3], beyond(up_ref))
        if row >= rows:
            return kept(z_ref[4], beyond(down_ref))
        return inside(row)

    for h in (0, rows - 1):
        blocks = input_row(
            lambda b: pick(h, b, lambda ref: ref[1 : planes + 1], lambda row: grad_ref[row]),
            lambda b: pick(h, b, lambda ref: kept(z_ref[1], ref[0]), lambda row: kept(z_ref[1], low_ref[row])),
            lambda b: pick(h, b, lambda ref: kept(z_ref[2], ref[planes + 1]), lambda row: kept(z_ref[2], high_ref[row])),
            weights_ref,
            hold_ref,
            offsets,
        )
        for out, block in zip(outs, blocks):
            out[h] = block


def call(kernel, outs, scratch, flops, args, scalar):
    nbytes = sum(math.prod(a.shape) * a.dtype.itemsize for a in list(args) + list(outs))
    return pl.pallas_call(
        kernel,
        out_shape=outs,
        in_specs=[pl.BlockSpec(memory_space=pltpu.SMEM)]
        + [pl.BlockSpec(memory_space=pltpu.VMEM)] * len(args),
        out_specs=[pl.BlockSpec(memory_space=pltpu.VMEM)] * len(outs),
        scratch_shapes=scratch,
        compiler_params=pltpu.CompilerParams(vmem_limit_bytes=VMEM_BYTES),
        cost_estimate=pl.CostEstimate(
            flops=flops, bytes_accessed=nbytes if flops else 0, transcendentals=0
        ),
    )(scalar, *args)


def row_blocks(array, halo, z, chan_count):
    turned = jnp.pad(array.transpose(2, 1, 0, 3), ((halo, halo), (0, 0), (0, 0), (0, 0)))
    rows = array.shape[2] // chan_count
    return [
        lax.dynamic_slice_in_dim(turned, lax.rem(z + j, chan_count) * rows, rows + 2 * halo, axis=0)
        for j in range(chan_count)
    ]


def exchange(blocks, axis):
    count = len(blocks)
    return [blocks[0]] + [
        lax.ppermute(blocks[j], axis, ring(count, j)) for j in range(1, count)
    ]


def after(value, *others):
    return lax.optimization_barrier((value, *others))[0]


def gather_filters(filters, z, s, chan_count, space_count):
    offsets, group, channels = filters.shape
    rows = offsets * group
    shard = -(-rows // (16 * space_count)) * 16
    flat = jnp.pad(filters.reshape(rows, channels), ((0, space_count * shard - rows), (0, 0)))
    mine = lax.dynamic_slice_in_dim(flat, s * shard, shard, axis=0)
    got = [mine] + [
        lax.ppermute(mine, "chan", ring(chan_count, j)) for j in range(1, chan_count)
    ]
    doubled = jnp.stack(got[::-1] + got[::-1])
    shares = lax.dynamic_slice_in_dim(doubled, chan_count - 1 - z, chan_count, axis=0)
    whole = lax.all_gather(shares, "space", axis=1, tiled=True)
    return whole[:, :rows].reshape(chan_count, offsets, group, channels)


def body(inputs, filters, cotangent):
    chan_count = lax.axis_size("chan")
    space_count = lax.axis_size("space")
    group, planes, height, cells = inputs.shape
    channels = group * chan_count
    rows = height // chan_count
    z = lax.axis_index("chan").astype(jnp.int32)
    s = lax.axis_index("space").astype(jnp.int32)
    upward, downward = ring(space_count, 1), ring(space_count, -1)
    shape = jax.ShapeDtypeStruct
    z_arg = jnp.stack(
        [z]
        + [
            flag.astype(jnp.int32)
            for flag in (s > 0, s < space_count - 1, z > 0, z < chan_count - 1)
        ]
    )

    x_pieces = exchange(row_blocks(inputs, 1, z, chan_count), "chan")
    filter_all = gather_filters(filters, z, s, chan_count, space_count)
    by_offset = filter_all.reshape(chan_count, 9, 3, group, channels)
    weights_f = by_offset.transpose(1, 0, 3, 2, 4).reshape(9 * channels, 3 * channels)
    weights_b = by_offset.transpose(1, 4, 2, 0, 3).reshape(9 * channels, 3 * channels)
    first, second, *rest = x_pieces
    second = after(second, weights_f)
    x_pieces = [first, second, *rest]

    x_top = jnp.concatenate([p[:, planes - 1 :] for p in x_pieces], axis=2)
    x_bottom = jnp.concatenate([p[:, :1] for p in x_pieces], axis=2)
    x_low = lax.ppermute(x_top, "space", upward)
    x_high = lax.ppermute(x_bottom, "space", downward)
    c_blocks = row_blocks(cotangent, 0, z, chan_count)
    c_pieces = exchange(
        c_blocks[:1] + [after(c, x) for c, x in zip(c_blocks[1:], x_pieces[1:])], "chan"
    )

    macs = 27 * channels * channels * rows * planes * cells
    padded = (rows + 2, planes + 2, channels, cells)
    plane = shape((rows, cells, channels), BF16)
    slope, x_first = call(
        functools.partial(forward_kernel, chan_count),
        [shape((rows, planes, cells, channels), F32), shape(padded, BF16)],
        [pltpu.VMEM((rows + 2, planes + 2, cells, channels), BF16)],
        0,
        [*x_pieces, x_low, x_high, weights_f],
        z_arg,
    )
    grad, g_bottom, g_top = call(
        functools.partial(grad_out_kernel, chan_count),
        [shape((rows, planes, cells, channels), BF16), plane, plane],
        [pltpu.VMEM((planes, channels, cells), BF16)],
        10 * rows * planes * cells * channels,
        [*c_pieces, slope],
        z_arg,
    )
    g_low = lax.ppermute(g_top, "space", upward)
    g_high = lax.ppermute(g_bottom, "space", downward)

    chips = space_count // 2
    shard = -(-27 * group // (16 * space_count)) * 16
    half = shape((chips, chan_count, shard, channels), F32)
    keep, send = call(
        functools.partial(filter_kernel, chan_count, space_count, shard),
        [half, half],
        [
            pltpu.VMEM((9 * channels, 3 * channels), F32),
            pltpu.VMEM((chan_count, space_count * shard, channels), F32),
        ],
        6 * macs,
        [x_first, grad],
        lax.rem(s, 2).reshape(1),
    )
    from_core = lax.ppermute(send, "space", [(i, i ^ 1) for i in range(space_count)])
    pair_sum = keep + from_core
    edges = [
        jnp.concatenate([g_low[r : r + 1], grad[r], g_high[r : r + 1]], axis=0)
        for r in (rows - 1, 0)
    ]
    g_up = lax.ppermute(edges[0], "chan", ring(chan_count, 1))
    g_down = lax.ppermute(edges[1], "chan", ring(chan_count, -1))
    chip = s // 2
    chip_sum = lax.dynamic_index_in_dim(pair_sum, chip, 0, keepdims=False)
    rounded = pair_sum.astype(BF16)
    from_chips = []
    for k in range(1, chips):
        block = lax.dynamic_index_in_dim(rounded, chip ^ k, 0, keepdims=False)
        from_chips.append(
            lax.ppermute(block, "space", [(i, i ^ (2 * k)) for i in range(space_count)])
        )
    g_low, g_high = after((g_low, g_high), rounded)
    inner = call(
        functools.partial(inner_kernel, chan_count),
        [shape((rows - 2, planes, group, cells), BF16)] * chan_count,
        [pltpu.VMEM((planes, channels, cells), BF16)],
        5 * macs,
        [grad, g_low, g_high, weights_b],
        z_arg,
    )
    g_up, g_down, from_chips = after((g_up, g_down, from_chips), inner[0])
    for got in from_chips:
        chip_sum = chip_sum + got.astype(F32)
    parts = [
        lax.dynamic_index_in_dim(chip_sum, lax.rem(z + j, chan_count), 0, keepdims=False)
        for j in range(chan_count)
    ]
    g_up, g_down = after((g_up, g_down), parts)
    back = call(
        functools.partial(edge_kernel, chan_count),
        [shape((rows, planes, group, cells), BF16)] * chan_count,
        [pltpu.VMEM((planes, channels, cells), BF16)],
        2 * macs,
        [grad, g_low, g_high, g_up, g_down, weights_b, *inner],
        z_arg,
    )
    returned = exchange(back, "chan")

    summed = exchange(parts, "chan")
    shard_sum = sum(after(summed, back[0]))
    cell_total = planes * space_count * height * cells
    shard_sum = shard_sum * (1.0 / math.sqrt(cell_total))
    returned = after(returned, shard_sum)
    whole = lax.all_gather(shard_sum, "space", axis=0, tiled=True)
    grad_w = whole[: 27 * group].reshape(27, group, channels)

    reverse = returned[::-1]
    doubled = jnp.concatenate(reverse + reverse, axis=0)
    start = lax.rem(chan_count - 1 - z + chan_count, chan_count) * rows
    ordered = lax.dynamic_slice_in_dim(doubled, start, height, axis=0)
    return ordered.transpose(2, 1, 0, 3), grad_w


def solution(mesh):
    placed = (P("chan", "space", None, None), P(None, "chan", None), P("chan", "space", None, None))
    return jax.shard_map(
        body,
        mesh=mesh,
        in_specs=placed,
        out_specs=(P("chan", "space", None, None), P(None, "chan", None)),
        check_vma=False,
    )
```

```python
import functools
import math

import jax
import jax.numpy as jnp
from jax import lax
from jax.experimental import pallas as pl
from jax.experimental.pallas import tpu as pltpu
from jax.sharding import PartitionSpec as P

BF16 = jnp.bfloat16
F32 = jnp.float32
VMEM_BYTES = 56 * 1024 * 1024


def ring(count, step):
    return [(i, (i + step) % count) for i in range(count)]


def after(value, *others):
    return lax.optimization_barrier((value, *others))[0]


def kept(flag, value):
    return jnp.where(flag > 0, value, jnp.zeros_like(value))


def window(mid, low, high, a, height):
    if a == 0:
        return jnp.concatenate([low, mid[:, :-height]], axis=1)
    if a == 2:
        return jnp.concatenate([mid[:, height:], high], axis=1)
    return mid


def row_shifts(value, height):
    split = value.reshape(-1, height, value.shape[-1])
    row = lax.broadcasted_iota(jnp.int32, split.shape, 1)
    later = jnp.where(row == height - 1, 0.0, pltpu.roll(split, height - 1, 1))
    earlier = jnp.where(row == 0, 0.0, pltpu.roll(split, 1, 1))
    return later.reshape(value.shape), earlier.reshape(value.shape)


def convolve(columns, weights, channels, height, mirrored):
    lhs = jnp.concatenate([c.reshape(-1, channels) for c in columns], axis=1)
    out = jnp.dot(lhs, weights, preferred_element_type=F32)
    first, mid, last = (out[:, t * channels : (t + 1) * channels] for t in range(3))
    if mirrored:
        first, last = last, first
    return mid + row_shifts(first, height)[1] + row_shifts(last, height)[0]


def group_offsets(z, chan_count, group, sign):
    return [
        pl.multiple_of(lax.rem(z + sign * j + chan_count, chan_count) * group, group)
        for j in range(chan_count)
    ]


def block_step(rows):
    return max(1, 1024 // rows)


def over_columns(count, rows, visit):
    step = block_step(rows)
    loops, rest = count // step, count % step
    if loops:
        pl.loop(0, loops)(lambda i: visit(i * step, step))
    if rest:
        visit(loops * step, rest)


def turn_kernel(chan_count, height, z_ref, *refs):
    pieces = refs[:chan_count]
    first_ref, cells_ref, bottom_ref, top_ref = refs[chan_count:]
    columns, group, cells = pieces[0].shape
    offsets = group_offsets(z_ref[0], chan_count, group, -1)

    def visit(k, count):
        for n in range(count):
            for j in range(chan_count):
                first_ref[k + n, pl.ds(offsets[j], group), :] = pieces[j][k + n]
        for n in range(count):
            tile = first_ref[k + n].T
            cells_ref[k + n] = tile
            bottom_ref[k + n] = tile[:height]
            top_ref[k + n] = tile[cells - height :]

    over_columns(columns, cells, visit)


def weights_kernel(_, weights_ref, out_ref):
    size = weights_ref.shape[1] // 3
    for k in range(9):
        for t in range(3):
            tile = (slice(k * size, (k + 1) * size), slice(t * size, (t + 1) * size))
            out_ref[tile] = weights_ref[tile].T


def slope_of(pre):
    sigma = 1.0 / (1.0 + jnp.exp(-pre))
    return sigma * (1.0 + pre * (1.0 - sigma))


def forward_inner_kernel(height, _, x_ref, weights_ref, slope_ref):
    columns, cells, channels = slope_ref.shape

    def visit(k, count):
        parts = [
            x_ref[pl.ds(k + b, count), a * height : a * height + cells]
            for a in range(3)
            for b in range(3)
        ]
        pre = convolve(parts, weights_ref[...], channels, height, False)
        slope_ref[pl.ds(k, count)] = slope_of(pre).reshape(count, cells, channels)

    over_columns(columns, cells, visit)


def forward_outer_kernel(z_ref, x_ref, low_ref, high_ref, weights_ref, slope_ref):
    columns, cells, channels = slope_ref.shape
    height = cells // 2
    top = x_ref.shape[1]

    def visit(k, count):
        parts = []
        for a in range(3):
            for b in range(3):
                near = pl.ds(k + b, count)
                if a == 0:
                    first = kept(z_ref[1], low_ref[near])
                else:
                    first = x_ref[near, (a - 1) * height : a * height]
                if a == 2:
                    last = kept(z_ref[2], high_ref[near])
                else:
                    last = x_ref[near, top - (2 - a) * height : top - (1 - a) * height]
                parts.append(jnp.concatenate([first, last], axis=1))
        pre = convolve(parts, weights_ref[...], channels, height, False)
        slope_ref[pl.ds(k, count)] = slope_of(pre).reshape(count, cells, channels)

    over_columns(columns, cells, visit)


def windows_kernel(z_ref, x_ref, low_ref, high_ref, out_ref):
    columns, _, cells = out_ref.shape[1:]
    height = low_ref.shape[1]

    def visit(k, count):
        for n in range(count):
            mid = x_ref[pl.ds(k + n + 1, 1)]
            low = kept(z_ref[1], low_ref[pl.ds(k + n + 1, 1)])
            high = kept(z_ref[2], high_ref[pl.ds(k + n + 1, 1)])
            out_ref[0, k + n] = window(mid, low, high, 0, height)[0].T
            out_ref[1, k + n] = window(mid, low, high, 2, height)[0].T

    over_columns(columns, cells, visit)


def grad_out_kernel(chan_count, height, z_ref, *refs):
    pieces = refs[:chan_count]
    inner_ref, outer_ref, grad_ref, bottom_ref, top_ref, hold_ref = refs[chan_count:]
    group = pieces[0].shape[1]
    columns, cells, _ = grad_ref.shape
    offsets = group_offsets(z_ref[0], chan_count, group, -1)

    def visit(k, count):
        for n in range(count):
            for j in range(chan_count):
                hold_ref[n, pl.ds(offsets[j], group), :] = pieces[j][k + n]
        for n in range(count):
            cot = hold_ref[n].T.astype(F32)
            outer = outer_ref[k + n]
            slope = jnp.concatenate([outer[:height], inner_ref[k + n], outer[height:]], axis=0)
            grad = (cot * slope).astype(BF16)
            grad_ref[k + n] = grad
            bottom_ref[k + n] = grad[:height]
            top_ref[k + n] = grad[cells - height :]

    over_columns(columns, cells, visit)


def filter_kernel(
    chan_count, space_count, shard, height, core_ref, x_ref, sides_ref, grad_ref, keep_ref, send_ref, acc_ref, pack_ref
):
    columns, cells, channels = grad_ref.shape
    group = channels // chan_count
    acc_ref[...] = jnp.zeros_like(acc_ref)

    def visit(k, count):
        lhs = jnp.concatenate(
            [
                jnp.concatenate(
                    [
                        x_ref[k + n + b + 1] if a == 1 else sides_ref[a // 2, k + n + b]
                        for n in range(count)
                    ],
                    axis=1,
                )
                for a in range(3)
                for b in range(3)
            ],
            axis=0,
        )
        grad = grad_ref[pl.ds(k + 1, count)].reshape(count * cells, channels).astype(F32)
        later, earlier = row_shifts(grad, height)
        rhs = jnp.concatenate([v.astype(BF16) for v in (later, grad, earlier)], axis=1)
        acc_ref[...] += jnp.dot(lhs, rhs, preferred_element_type=F32)

    over_columns(columns - 2, cells, visit)
    used = 27 * group
    for z in range(chan_count):
        for offset in range(27):
            a, t, m = offset // 9, offset // 3 % 3, offset % 3
            row = (3 * a + m) * channels + z * group
            pack_ref[z, offset * group : (offset + 1) * group, :] = acc_ref[
                row : row + group, t * channels : (t + 1) * channels
            ]
        pack_ref[z, used:, :] = jnp.zeros((space_count * shard - used, channels), F32)
    core = core_ref[0]
    for chip in range(space_count // 2):
        mine = pl.multiple_of((2 * chip + core) * shard, 8)
        other = pl.multiple_of((2 * chip + 1 - core) * shard, 8)
        for z in range(chan_count):
            keep_ref[chip, z] = pack_ref[z, pl.ds(mine, shard), :]
            send_ref[chip, z] = pack_ref[z, pl.ds(other, shard), :]


def input_kernel(chan_count, base, made, z_ref, grad_ref, low_ref, high_ref, weights_ref, *refs):
    earlier, outs, hold_ref = refs[: -1 - chan_count], refs[-1 - chan_count : -1], refs[-1]
    for out, old in zip(outs, earlier):
        out[:made] = old[...]
    columns, cells, channels = grad_ref.shape
    height = low_ref.shape[1]
    group = channels // chan_count
    offsets = group_offsets(z_ref[0], chan_count, group, 1)

    def visit(k, count):
        parts = [
            window(
                grad_ref[pl.ds(base + k + 2 - b, count)],
                kept(z_ref[1], low_ref[pl.ds(base + k + 2 - b, count)]),
                kept(z_ref[2], high_ref[pl.ds(base + k + 2 - b, count)]),
                2 - a,
                height,
            )
            for a in range(3)
            for b in range(3)
        ]
        total = convolve(parts, weights_ref[...], channels, height, True).astype(BF16)
        total = total.reshape(count, cells, channels)
        for n in range(count):
            hold_ref[n] = total[n].T
        for j in range(chan_count):
            for n in range(count):
                outs[j][made + k + n] = hold_ref[n, pl.ds(offsets[j], group), :]

    over_columns(outs[0].shape[0] - made, cells, visit)


def call(kernel, outs, scratch, flops, args, scalar):
    nbytes = sum(math.prod(a.shape) * a.dtype.itemsize for a in list(args) + list(outs))
    return pl.pallas_call(
        kernel,
        out_shape=outs,
        in_specs=[pl.BlockSpec(memory_space=pltpu.SMEM)]
        + [pl.BlockSpec(memory_space=pltpu.VMEM)] * len(args),
        out_specs=[pl.BlockSpec(memory_space=pltpu.VMEM)] * len(outs),
        scratch_shapes=scratch,
        compiler_params=pltpu.CompilerParams(vmem_limit_bytes=VMEM_BYTES),
        cost_estimate=pl.CostEstimate(
            flops=flops, bytes_accessed=nbytes if flops else 0, transcendentals=0
        ),
    )(scalar, *args)


def column_blocks(array, before, behind, z, chan_count):
    group, planes, height, width = array.shape
    turned = array.reshape(group, planes * height, width).transpose(2, 0, 1)
    turned = jnp.pad(turned, ((before, behind), (0, 0), (0, 0)))
    columns = width // chan_count
    return [
        lax.dynamic_slice_in_dim(
            turned, lax.rem(z + j, chan_count) * columns, columns + before + behind, axis=0
        )
        for j in range(chan_count)
    ]


def exchange(blocks, axis):
    count = len(blocks)
    return [blocks[0]] + [
        lax.ppermute(blocks[j], axis, ring(count, j)) for j in range(1, count)
    ]


def gather_filters(filters, z, s, chan_count, space_count, shard):
    offsets, group, channels = filters.shape
    rows = offsets * group
    flat = jnp.pad(filters.reshape(rows, channels), ((0, space_count * shard - rows), (0, 0)))
    mine = lax.dynamic_slice_in_dim(flat, s * shard, shard, axis=0)
    got = [mine] + [
        lax.ppermute(mine, "chan", ring(chan_count, j)) for j in range(1, chan_count)
    ]
    doubled = jnp.stack(got[::-1] + got[::-1])
    shares = lax.dynamic_slice_in_dim(doubled, chan_count - 1 - z, chan_count, axis=0)
    whole = lax.all_gather(shares, "space", axis=1, tiled=True)
    return whole[:, :rows].reshape(chan_count, 3, 3, 3, group, channels)


def body(inputs, filters, cotangent):
    chan_count = lax.axis_size("chan")
    space_count = lax.axis_size("space")
    group, planes, height, width = inputs.shape
    channels = group * chan_count
    columns = width // chan_count
    cells = planes * height
    z = lax.axis_index("chan").astype(jnp.int32)
    s = lax.axis_index("space").astype(jnp.int32)
    upward, downward = ring(space_count, 1), ring(space_count, -1)
    shape = jax.ShapeDtypeStruct
    flags = [(s > 0).astype(jnp.int32), (s < space_count - 1).astype(jnp.int32)]
    z_arg = jnp.stack([z] + flags)
    macs = 27 * channels * channels * columns * cells

    x_pieces = exchange(column_blocks(inputs, 2, 2, z, chan_count), "chan")
    shard = -(-27 * group // (16 * space_count)) * 16
    by_offset = gather_filters(filters, z, s, chan_count, space_count, shard)
    weights_f = by_offset.transpose(1, 3, 0, 4, 2, 5).reshape(9 * channels, 3 * channels)
    c_blocks = column_blocks(cotangent, 1, 4, z, chan_count)
    weights_b = call(
        weights_kernel, [shape(weights_f.shape, BF16)], [], 0, [weights_f], z_arg
    )[0]
    x_pieces = after(x_pieces, weights_b, z_arg, c_blocks)

    x_first, x_cells, x_bottom, x_top = call(
        functools.partial(turn_kernel, chan_count, height),
        [
            shape((columns + 4, channels, cells), BF16),
            shape((columns + 4, cells, channels), BF16),
        ]
        + [shape((columns + 4, height, channels), BF16)] * 2,
        [],
        0,
        x_pieces,
        z_arg,
    )
    x_low = lax.ppermute(x_top, "space", upward)
    x_high = lax.ppermute(x_bottom, "space", downward)
    c_pieces = exchange(
        c_blocks[:1] + [after(c, x) for c, x in zip(c_blocks[1:], x_pieces[1:])], "chan"
    )
    slope_inner = call(
        functools.partial(forward_inner_kernel, height),
        [shape((columns + 2, cells - 2 * height, channels), F32)],
        [],
        0,
        [x_cells, weights_f],
        z_arg,
    )[0]
    slope_outer = call(
        forward_outer_kernel,
        [shape((columns + 2, 2 * height, channels), F32)],
        [],
        0,
        [after(x_cells, slope_inner), x_low, x_high, weights_f],
        z_arg,
    )[0]
    x_windows = call(
        windows_kernel,
        [shape((2, columns + 2, channels, cells), BF16)],
        [],
        0,
        [x_cells, x_low, x_high],
        z_arg,
    )[0]
    slope_outer = after(slope_outer, x_windows)
    grad, g_bottom, g_top = call(
        functools.partial(grad_out_kernel, chan_count, height),
        [shape((columns + 2, cells, channels), BF16)]
        + [shape((columns + 2, height, channels), BF16)] * 2,
        [pltpu.VMEM((block_step(cells), channels, cells), BF16)],
        10 * columns * cells * channels,
        [*c_pieces, slope_inner, slope_outer],
        z_arg,
    )
    g_low = lax.ppermute(g_top, "space", upward)
    g_high = lax.ppermute(g_bottom, "space", downward)

    chips = space_count // 2
    half = shape((chips, chan_count, shard, channels), F32)
    keep, send = call(
        functools.partial(filter_kernel, chan_count, space_count, shard, height),
        [half, half],
        [
            pltpu.VMEM((9 * channels, 3 * channels), F32),
            pltpu.VMEM((chan_count, space_count * shard, channels), F32),
        ],
        0,
        [x_first, x_windows, grad],
        lax.rem(s, 2).reshape(1),
    )
    g_low, g_high, send = lax.optimization_barrier((g_low, g_high, send))
    from_core = lax.ppermute(send, "space", [(i, i ^ 1) for i in range(space_count)])
    half_columns = columns // 2
    hold = [pltpu.VMEM((block_step(cells), channels, cells), BF16)]
    first = call(
        functools.partial(input_kernel, chan_count, 0, 0),
        [shape((half_columns, group, cells), BF16)] * chan_count,
        hold,
        3 * macs,
        [grad, g_low, g_high, weights_b],
        z_arg,
    )
    pair_sum = keep + after(from_core, first[0])
    chip = s // 2
    chip_sum = lax.dynamic_index_in_dim(pair_sum, chip, 0, keepdims=False)
    rounded = pair_sum.astype(BF16)
    g_low, g_high = after((g_low, g_high), rounded)
    from_chips = []
    for k in range(1, chips):
        block = lax.dynamic_index_in_dim(rounded, chip ^ k, 0, keepdims=False)
        from_chips.append(
            lax.ppermute(block, "space", [(i, i ^ (2 * k)) for i in range(space_count)])
        )
    back = call(
        functools.partial(input_kernel, chan_count, half_columns, half_columns),
        [shape((columns, group, cells), BF16)] * chan_count,
        hold,
        3 * macs,
        [grad, g_low, g_high, weights_b, *first],
        z_arg,
    )
    returned = exchange(back, "chan")
    for got in after(from_chips, back[0]):
        chip_sum = chip_sum + got.astype(F32)
    parts = [
        lax.dynamic_index_in_dim(chip_sum, lax.rem(z + j, chan_count), 0, keepdims=False)
        for j in range(chan_count)
    ]
    shard_sum = sum(exchange(parts, "chan"))
    returned = after(returned, shard_sum)
    cell_total = planes * space_count * height * width
    shard_sum = shard_sum * (1.0 / math.sqrt(cell_total))
    whole = lax.all_gather(shard_sum, "space", axis=0, tiled=True)
    grad_w = whole[: 27 * group].reshape(27, group, channels)

    reverse = returned[::-1]
    doubled = jnp.concatenate(reverse + reverse, axis=0)
    start = lax.rem(chan_count - 1 - z + chan_count, chan_count) * columns
    ordered = lax.dynamic_slice_in_dim(doubled, start, width, axis=0)
    return ordered.transpose(1, 2, 0).reshape(group, planes, height, width), grad_w


def solution(mesh):
    placed = (P("chan", "space", None, None), P(None, "chan", None), P("chan", "space", None, None))
    return jax.shard_map(
        body,
        mesh=mesh,
        in_specs=placed,
        out_specs=(P("chan", "space", None, None), P(None, "chan", None)),
        check_vma=False,
    )
```

```python
import functools
import math

import jax
import jax.numpy as jnp
from jax import lax
from jax.experimental import pallas as pl
from jax.experimental.pallas import tpu as pltpu
from jax.sharding import PartitionSpec as P

BF16 = jnp.bfloat16
F32 = jnp.float32
VMEM_BYTES = 56 * 1024 * 1024


def ring(count, step):
    return [(i, (i + step) % count) for i in range(count)]


def after(value, *others):
    return lax.optimization_barrier((value, *others))[0]


def kept(flag, value):
    return jnp.where(flag > 0, value, jnp.zeros_like(value))


def window(mid, low, high, a, height):
    if a == 0:
        return jnp.concatenate([low, mid[:, :-height]], axis=1)
    if a == 2:
        return jnp.concatenate([mid[:, height:], high], axis=1)
    return mid


def row_shifts(value, height):
    split = value.reshape(-1, height, value.shape[-1])
    row = lax.broadcasted_iota(jnp.int32, split.shape, 1)
    later = jnp.where(row == height - 1, 0.0, pltpu.roll(split, height - 1, 1))
    earlier = jnp.where(row == 0, 0.0, pltpu.roll(split, 1, 1))
    return later.reshape(value.shape), earlier.reshape(value.shape)


def convolve(columns, weights, channels, height, mirrored):
    lhs = jnp.concatenate([c.reshape(-1, channels) for c in columns], axis=1)
    out = jnp.dot(lhs, weights, preferred_element_type=F32)
    first, mid, last = (out[:, t * channels : (t + 1) * channels] for t in range(3))
    if mirrored:
        first, last = last, first
    return mid + row_shifts(first, height)[1] + row_shifts(last, height)[0]


def group_offsets(z, chan_count, group, sign):
    return [
        pl.multiple_of(lax.rem(z + sign * j + chan_count, chan_count) * group, group)
        for j in range(chan_count)
    ]


def pair_offsets(z, chan_count, group):
    return [pl.multiple_of((z ^ j) * group, group) for j in range(chan_count)]


def block_step(rows):
    return max(1, 1024 // rows)


def over_columns(count, rows, visit):
    step = block_step(rows)
    loops, rest = count // step, count % step
    if loops:
        pl.loop(0, loops)(lambda i: visit(i * step, step))
    if rest:
        visit(loops * step, rest)


def turn_kernel(chan_count, height, z_ref, *refs):
    pieces = refs[:chan_count]
    first_ref, cells_ref, bottom_ref, top_ref = refs[chan_count:]
    columns, group, cells = pieces[0].shape
    offsets = pair_offsets(z_ref[0], chan_count, group)

    def visit(k, count):
        for n in range(count):
            for j in range(chan_count):
                first_ref[k + n, pl.ds(offsets[j], group), :] = pieces[j][k + n]
        for n in range(count):
            tile = first_ref[k + n].T
            cells_ref[k + n] = tile
            bottom_ref[k + n] = tile[:height]
            top_ref[k + n] = tile[cells - height :]

    over_columns(columns, cells, visit)


def share_plan(chan_count, space_count, rows):
    far = chan_count - 1
    plan = [(s % far + 1, s // far) for s in range(space_count)]
    counts = [0] + [sum(step == k for step, _ in plan) for k in range(1, chan_count)]
    return plan, [0] + [-(-rows // (16 * n)) * 16 for n in counts[1:]]


def weights_kernel(chan_count, z_ref, own_ref, shares_ref, forward_ref, backward_ref):
    offsets, group, channels = own_ref.shape
    plan, sizes = share_plan(chan_count, shares_ref.shape[0], offsets * group)
    places = group_offsets(z_ref[0], chan_count, group, -1)
    for offset in range(offsets):
        a, t, m = offset // 9, offset // 3 % 3, offset % 3
        for j in range(chan_count):
            for i in range(0, group, 16):
                if j == 0:
                    rows = own_ref[offset, i : i + 16]
                else:
                    source = offset * group + i
                    part, row = divmod(source, sizes[j])
                    rows = shares_ref[plan.index((j, part)), row : row + 16]
                row = pl.multiple_of((3 * a + m) * channels + places[j] + i, 16)
                forward_ref[pl.ds(row, 16), t * channels : (t + 1) * channels] = rows
    for k in range(9):
        for t in range(3):
            tile = (
                slice(k * channels, (k + 1) * channels),
                slice(t * channels, (t + 1) * channels),
            )
            backward_ref[tile] = forward_ref[tile].T


def slope_of(pre):
    sigma = 1.0 / (1.0 + jnp.exp(-pre))
    return sigma * (1.0 + pre * (1.0 - sigma))


def forward_inner_kernel(height, _, x_ref, weights_ref, slope_ref):
    columns, cells, channels = slope_ref.shape

    def visit(k, count):
        parts = [
            x_ref[pl.ds(k + b, count), a * height : a * height + cells]
            for a in range(3)
            for b in range(3)
        ]
        pre = convolve(parts, weights_ref[...], channels, height, False)
        slope_ref[pl.ds(k, count)] = slope_of(pre).reshape(count, cells, channels)

    over_columns(columns, cells, visit)


def forward_outer_kernel(z_ref, x_ref, low_ref, high_ref, weights_ref, slope_ref):
    columns, cells, channels = slope_ref.shape
    height = cells // 2
    top = x_ref.shape[1]

    def visit(k, count):
        parts = []
        for a in range(3):
            for b in range(3):
                near = pl.ds(k + b, count)
                if a == 0:
                    first = kept(z_ref[1], low_ref[near])
                else:
                    first = x_ref[near, (a - 1) * height : a * height]
                if a == 2:
                    last = kept(z_ref[2], high_ref[near])
                else:
                    last = x_ref[near, top - (2 - a) * height : top - (1 - a) * height]
                parts.append(jnp.concatenate([first, last], axis=1))
        pre = convolve(parts, weights_ref[...], channels, height, False)
        slope_ref[pl.ds(k, count)] = slope_of(pre).reshape(count, cells, channels)

    over_columns(columns, cells, visit)


def windows_kernel(z_ref, x_ref, low_ref, high_ref, out_ref):
    columns, _, cells = out_ref.shape[1:]
    height = low_ref.shape[1]

    def visit(k, count):
        for n in range(count):
            mid = x_ref[pl.ds(k + n + 1, 1)]
            low = kept(z_ref[1], low_ref[pl.ds(k + n + 1, 1)])
            high = kept(z_ref[2], high_ref[pl.ds(k + n + 1, 1)])
            out_ref[0, k + n] = window(mid, low, high, 0, height)[0].T
            out_ref[1, k + n] = window(mid, low, high, 2, height)[0].T

    over_columns(columns, cells, visit)


def grad_out_kernel(chan_count, height, z_ref, *refs):
    pieces = refs[:chan_count]
    inner_ref, outer_ref, grad_ref, bottom_ref, top_ref, hold_ref = refs[chan_count:]
    group = pieces[0].shape[1]
    columns, cells, _ = grad_ref.shape
    offsets = pair_offsets(z_ref[0], chan_count, group)

    def visit(k, count):
        for n in range(count):
            for j in range(chan_count):
                hold_ref[n, pl.ds(offsets[j], group), :] = pieces[j][k + n]
        for n in range(count):
            cot = hold_ref[n].T.astype(F32)
            outer = outer_ref[k + n]
            slope = jnp.concatenate([outer[:height], inner_ref[k + n], outer[height:]], axis=0)
            grad = (cot * slope).astype(BF16)
            grad_ref[k + n] = grad
            bottom_ref[k + n] = grad[:height]
            top_ref[k + n] = grad[cells - height :]

    over_columns(columns, cells, visit)


def filter_kernel(
    chan_count, space_count, shard, height, core_ref, x_ref, sides_ref, grad_ref, keep_ref, send_ref, acc_ref, pack_ref
):
    columns, cells, channels = grad_ref.shape
    group = channels // chan_count
    acc_ref[...] = jnp.zeros_like(acc_ref)

    def visit(k, count):
        lhs = jnp.concatenate(
            [
                jnp.concatenate(
                    [
                        x_ref[k + n + b + 1] if a == 1 else sides_ref[a // 2, k + n + b]
                        for n in range(count)
                    ],
                    axis=1,
                )
                for a in range(3)
                for b in range(3)
            ],
            axis=0,
        )
        grad = grad_ref[pl.ds(k + 1, count)].reshape(count * cells, channels).astype(F32)
        later, earlier = row_shifts(grad, height)
        rhs = jnp.concatenate([v.astype(BF16) for v in (later, grad, earlier)], axis=1)
        acc_ref[...] += jnp.dot(lhs, rhs, preferred_element_type=F32)

    over_columns(columns - 2, cells, visit)
    used = 27 * group
    for z in range(chan_count):
        for offset in range(27):
            a, t, m = offset // 9, offset // 3 % 3, offset % 3
            row = (3 * a + m) * channels + z * group
            pack_ref[z, offset * group : (offset + 1) * group, :] = acc_ref[
                row : row + group, t * channels : (t + 1) * channels
            ]
        pack_ref[z, used:, :] = jnp.zeros((space_count * shard - used, channels), F32)
    core = core_ref[0]
    for chip in range(space_count // 2):
        mine = pl.multiple_of((2 * chip + core) * shard, 8)
        other = pl.multiple_of((2 * chip + 1 - core) * shard, 8)
        for z in range(chan_count):
            keep_ref[chip, z] = pack_ref[z, pl.ds(mine, shard), :]
            send_ref[chip, z] = pack_ref[z, pl.ds(other, shard), :]


def input_kernel(chan_count, base, count, z_ref, grad_ref, low_ref, high_ref, weights_ref, *refs):
    made, outs, hold_ref = refs[: -1 - chan_count], refs[-1 - chan_count : -1], refs[-1]
    starts = [out.shape[0] - count for out in outs]
    for out, old in zip([out for out, start in zip(outs, starts) if start], made):
        out[: old.shape[0]] = old[...]
    columns, cells, channels = grad_ref.shape
    height = low_ref.shape[1]
    group = channels // chan_count
    offsets = group_offsets(z_ref[0], chan_count, group, 1)

    def visit(k, width):
        parts = [
            window(
                grad_ref[pl.ds(base + k + 2 - b, width)],
                kept(z_ref[1], low_ref[pl.ds(base + k + 2 - b, width)]),
                kept(z_ref[2], high_ref[pl.ds(base + k + 2 - b, width)]),
                2 - a,
                height,
            )
            for a in range(3)
            for b in range(3)
        ]
        total = convolve(parts, weights_ref[...], channels, height, True).astype(BF16)
        total = total.reshape(width, cells, channels)
        for n in range(width):
            hold_ref[n] = total[n].T
        for j in range(chan_count):
            for n in range(width):
                outs[j][starts[j] + k + n] = hold_ref[n, pl.ds(offsets[j], group), :]

    over_columns(count, cells, visit)


def call(kernel, outs, scratch, flops, args, scalar):
    nbytes = sum(math.prod(a.shape) * a.dtype.itemsize for a in list(args) + list(outs))
    return pl.pallas_call(
        kernel,
        out_shape=outs,
        in_specs=[pl.BlockSpec(memory_space=pltpu.SMEM)]
        + [pl.BlockSpec(memory_space=pltpu.VMEM)] * len(args),
        out_specs=[pl.BlockSpec(memory_space=pltpu.VMEM)] * len(outs),
        scratch_shapes=scratch,
        compiler_params=pltpu.CompilerParams(vmem_limit_bytes=VMEM_BYTES),
        cost_estimate=pl.CostEstimate(
            flops=flops, bytes_accessed=nbytes if flops else 0, transcendentals=0
        ),
    )(scalar, *args)


def column_blocks(array, before, behind, z, chan_count):
    group, planes, height, width = array.shape
    turned = array.reshape(group, planes * height, width).transpose(2, 0, 1)
    turned = jnp.pad(turned, ((before, behind), (0, 0), (0, 0)))
    columns = width // chan_count
    return [
        lax.dynamic_slice_in_dim(
            turned, (z ^ j) * columns, columns + before + behind, axis=0
        )
        for j in range(chan_count)
    ]


def swap(blocks):
    count = len(blocks)
    got = {
        j: lax.ppermute(blocks[j], "chan", [(i, i ^ j) for i in range(count)])
        for j in range(count - 1, 0, -1)
    }
    return [blocks[0]] + [got[j] for j in range(1, count)]


def exchange(blocks, axis):
    count = len(blocks)
    return [blocks[0]] + [
        lax.ppermute(blocks[j], axis, ring(count, j)) for j in range(1, count)
    ]


def fetch_filters(filters, s, chan_count, space_count):
    offsets, group, channels = filters.shape
    rows = offsets * group
    plan, sizes = share_plan(chan_count, space_count, rows)
    starts = [part * sizes[step] for step, part in plan]
    size = max(sizes)
    flat = jnp.pad(filters.reshape(rows, channels), ((0, max(starts) + size - rows), (0, 0)))
    far = chan_count - 1
    per_part = sum((s % far + 1 == k) * sizes[k] for k in range(1, chan_count))
    mine = lax.dynamic_slice_in_dim(flat, s // far * per_part, size, axis=0)
    route = [
        (place * chan_count + z, place * chan_count + (z + step) % chan_count)
        for place, (step, _) in enumerate(plan)
        for z in range(chan_count)
    ]
    return lax.ppermute(mine, ("space", "chan"), route)


def body(inputs, filters, cotangent):
    chan_count = lax.axis_size("chan")
    space_count = lax.axis_size("space")
    group, planes, height, width = inputs.shape
    channels = group * chan_count
    columns = width // chan_count
    cells = planes * height
    z = lax.axis_index("chan").astype(jnp.int32)
    s = lax.axis_index("space").astype(jnp.int32)
    upward, downward = ring(space_count, 1), ring(space_count, -1)
    shape = jax.ShapeDtypeStruct
    flags = [(s > 0).astype(jnp.int32), (s < space_count - 1).astype(jnp.int32)]
    z_arg = jnp.stack([z] + flags)
    macs = 27 * channels * channels * columns * cells

    share = fetch_filters(filters, s, chan_count, space_count)
    x_pieces = swap(after(column_blocks(inputs, 2, 2, z, chan_count), share))
    shares = lax.all_gather(share, "space", axis=0, tiled=False)
    c_blocks = column_blocks(after(cotangent, shares), 1, 4, z, chan_count)
    weights_f, weights_b = call(
        functools.partial(weights_kernel, chan_count),
        [shape((9 * channels, 3 * channels), BF16)] * 2,
        [],
        0,
        [filters, shares],
        z_arg,
    )
    x_pieces = after(x_pieces, weights_b, z_arg, c_blocks)

    x_first, x_cells, x_bottom, x_top = call(
        functools.partial(turn_kernel, chan_count, height),
        [
            shape((columns + 4, channels, cells), BF16),
            shape((columns + 4, cells, channels), BF16),
        ]
        + [shape((columns + 4, height, channels), BF16)] * 2,
        [],
        0,
        x_pieces,
        z_arg,
    )
    x_low = lax.ppermute(x_top, "space", upward)
    x_high = lax.ppermute(x_bottom, "space", downward)
    c_pieces = swap(c_blocks[:1] + [after(c, x) for c, x in zip(c_blocks[1:], x_pieces[1:])])
    slope_inner = call(
        functools.partial(forward_inner_kernel, height),
        [shape((columns + 2, cells - 2 * height, channels), F32)],
        [],
        0,
        [x_cells, weights_f],
        z_arg,
    )[0]
    slope_outer = call(
        forward_outer_kernel,
        [shape((columns + 2, 2 * height, channels), F32)],
        [],
        0,
        [after(x_cells, slope_inner), x_low, x_high, weights_f],
        z_arg,
    )[0]
    x_windows = call(
        windows_kernel,
        [shape((2, columns + 2, channels, cells), BF16)],
        [],
        0,
        [x_cells, x_low, x_high],
        z_arg,
    )[0]
    slope_outer = after(slope_outer, x_windows)
    grad, g_bottom, g_top = call(
        functools.partial(grad_out_kernel, chan_count, height),
        [shape((columns + 2, cells, channels), BF16)]
        + [shape((columns + 2, height, channels), BF16)] * 2,
        [pltpu.VMEM((block_step(cells), channels, cells), BF16)],
        10 * columns * cells * channels,
        [*c_pieces, slope_inner, slope_outer],
        z_arg,
    )
    g_low = lax.ppermute(g_top, "space", upward)
    g_high = lax.ppermute(g_bottom, "space", downward)

    chips = space_count // 2
    shard = -(-27 * group // (16 * space_count)) * 16
    half = shape((chips, chan_count, shard, channels), F32)
    keep, send = call(
        functools.partial(filter_kernel, chan_count, space_count, shard, height),
        [half, half],
        [
            pltpu.VMEM((9 * channels, 3 * channels), F32),
            pltpu.VMEM((chan_count, space_count * shard, channels), F32),
        ],
        0,
        [x_first, x_windows, grad],
        lax.rem(s, 2).reshape(1),
    )
    g_low, g_high, send = lax.optimization_barrier((g_low, g_high, send))
    from_core = lax.ppermute(send, "space", [(i, i ^ 1) for i in range(space_count)])
    early = columns // 2
    split = range(1, min(3, chan_count))
    hold = [pltpu.VMEM((block_step(cells), channels, cells), BF16)]
    first = call(
        functools.partial(input_kernel, chan_count, 0, early),
        [shape((early, group, cells), BF16)] * chan_count,
        hold,
        3 * macs,
        [grad, g_low, g_high, weights_b],
        z_arg,
    )
    returned_first = {j: lax.ppermute(first[j], "chan", ring(chan_count, j)) for j in split}
    pair_sum = keep + after(from_core, first[0])
    chip = s // 2
    chip_sum = lax.dynamic_index_in_dim(pair_sum, chip, 0, keepdims=False)
    rounded = pair_sum.astype(BF16)
    g_low, g_high = after((g_low, g_high), rounded)
    from_chips = []
    for k in range(1, chips):
        block = lax.dynamic_index_in_dim(rounded, chip ^ k, 0, keepdims=False)
        from_chips.append(
            lax.ppermute(block, "space", [(i, i ^ (2 * k)) for i in range(space_count)])
        )
    whole_blocks = [j for j in range(chan_count) if j not in split]
    back = call(
        functools.partial(input_kernel, chan_count, early, columns - early),
        [
            shape((columns if j in whole_blocks else columns - early, group, cells), BF16)
            for j in range(chan_count)
        ],
        hold,
        3 * macs,
        [grad, g_low, g_high, weights_b] + [first[j] for j in whole_blocks],
        z_arg,
    )
    returned = exchange(back, "chan")
    from_chips, returned_first = after((from_chips, returned_first), back[0])
    for got in from_chips:
        chip_sum = chip_sum + got.astype(F32)
    chip_sum = after(chip_sum, returned_first)
    parts = [
        lax.dynamic_index_in_dim(chip_sum, lax.rem(z + j, chan_count), 0, keepdims=False)
        for j in range(chan_count)
    ]
    shard_sum = sum(exchange(parts, "chan"))
    returned = after(returned, shard_sum)
    cell_total = planes * space_count * height * width
    shard_sum = shard_sum * (1.0 / math.sqrt(cell_total))
    whole = lax.all_gather(shard_sum, "space", axis=0, tiled=True)
    grad_w = whole[: 27 * group].reshape(27, group, channels)

    reverse = [
        part
        for j in range(chan_count)[::-1]
        for part in ([returned_first[j]] if j in split else []) + [returned[j]]
    ]
    doubled = jnp.concatenate(reverse + reverse, axis=0)
    start = lax.rem(chan_count - 1 - z + chan_count, chan_count) * columns
    ordered = lax.dynamic_slice_in_dim(doubled, start, width, axis=0)
    return ordered.transpose(1, 2, 0).reshape(group, planes, height, width), grad_w


def solution(mesh):
    placed = (P("chan", "space", None, None), P(None, "chan", None), P("chan", "space", None, None))
    return jax.shard_map(
        body,
        mesh=mesh,
        in_specs=placed,
        out_specs=(P("chan", "space", None, None), P(None, "chan", None)),
        check_vma=False,
    )
```

```python
import functools
import math

import jax
import jax.numpy as jnp
from jax import lax
from jax.experimental import pallas as pl
from jax.experimental.pallas import tpu as pltpu
from jax.sharding import PartitionSpec as P

BF16 = jnp.bfloat16
F32 = jnp.float32
VMEM_BYTES = 56 * 1024 * 1024


def ring(count, step):
    return [(i, (i + step) % count) for i in range(count)]


def after(value, *others):
    return lax.optimization_barrier((value, *others))[0]


def kept(flag, value):
    return jnp.where(flag > 0, value, jnp.zeros_like(value))


def window(mid, low, high, a, height):
    if a == 0:
        return jnp.concatenate([low, mid[:, :-height]], axis=1)
    if a == 2:
        return jnp.concatenate([mid[:, height:], high], axis=1)
    return mid


def row_shifts(value, height):
    split = value.reshape(-1, height, value.shape[-1])
    row = lax.broadcasted_iota(jnp.int32, split.shape, 1)
    later = jnp.where(row == height - 1, 0.0, pltpu.roll(split, height - 1, 1))
    earlier = jnp.where(row == 0, 0.0, pltpu.roll(split, 1, 1))
    return later.reshape(value.shape), earlier.reshape(value.shape)


def convolve(columns, weights, channels, height, mirrored):
    lhs = jnp.concatenate([c.reshape(-1, channels) for c in columns], axis=1)
    out = jnp.dot(lhs, weights, preferred_element_type=F32)
    first, mid, last = (out[:, t * channels : (t + 1) * channels] for t in range(3))
    if mirrored:
        first, last = last, first
    return mid + row_shifts(first, height)[1] + row_shifts(last, height)[0]


def group_offsets(z, chan_count, group, sign):
    return [
        pl.multiple_of(lax.rem(z + sign * j + chan_count, chan_count) * group, group)
        for j in range(chan_count)
    ]


def pair_offsets(z, chan_count, group):
    return [pl.multiple_of((z ^ j) * group, group) for j in range(chan_count)]


def block_step(rows):
    return max(1, 2048 // rows)


def over_columns(count, rows, visit):
    step = block_step(rows)
    loops, rest = count // step, count % step
    if loops:
        pl.loop(0, loops)(lambda i: visit(i * step, step))
    if rest:
        visit(loops * step, rest)


def turn_kernel(chan_count, height, z_ref, *refs):
    pieces = refs[:chan_count]
    first_ref, cells_ref, bottom_ref, top_ref = refs[chan_count:]
    columns, group, cells = pieces[0].shape
    offsets = pair_offsets(z_ref[0], chan_count, group)

    def visit(k, count):
        for n in range(count):
            for j in range(chan_count):
                first_ref[k + n, pl.ds(offsets[j], group), :] = pieces[j][k + n]
        for n in range(count):
            tile = first_ref[k + n].T
            cells_ref[k + n] = tile
            bottom_ref[k + n] = tile[:height]
            top_ref[k + n] = tile[cells - height :]

    over_columns(columns, cells, visit)


def share_plan(chan_count, space_count, rows):
    far = chan_count - 1
    plan = [(s % far + 1, s // far) for s in range(space_count)]
    counts = [0] + [sum(step == k for step, _ in plan) for k in range(1, chan_count)]
    return plan, [0] + [-(-rows // (16 * n)) * 16 for n in counts[1:]]


def weights_kernel(chan_count, z_ref, own_ref, shares_ref, forward_ref, backward_ref):
    offsets, group, channels = own_ref.shape
    plan, sizes = share_plan(chan_count, shares_ref.shape[0], offsets * group)
    places = group_offsets(z_ref[0], chan_count, group, -1)
    for offset in range(offsets):
        a, t, m = offset // 9, offset // 3 % 3, offset % 3
        for j in range(chan_count):
            for i in range(0, group, 16):
                if j == 0:
                    rows = own_ref[offset, i : i + 16]
                else:
                    source = offset * group + i
                    part, row = divmod(source, sizes[j])
                    rows = shares_ref[plan.index((j, part)), row : row + 16]
                row = pl.multiple_of((3 * a + m) * channels + places[j] + i, 16)
                forward_ref[pl.ds(row, 16), t * channels : (t + 1) * channels] = rows
    for k in range(9):
        for t in range(3):
            tile = (
                slice(k * channels, (k + 1) * channels),
                slice(t * channels, (t + 1) * channels),
            )
            backward_ref[tile] = forward_ref[tile].T


def slope_of(pre):
    sigma = 1.0 / (1.0 + jnp.exp(-pre))
    return sigma * (1.0 + pre * (1.0 - sigma))


def forward_inner_kernel(height, _, x_ref, weights_ref, slope_ref):
    columns, cells, channels = slope_ref.shape

    def visit(k, count):
        parts = [
            x_ref[pl.ds(k + b, count), a * height : a * height + cells]
            for a in range(3)
            for b in range(3)
        ]
        pre = convolve(parts, weights_ref[...], channels, height, False)
        slope_ref[pl.ds(k, count)] = slope_of(pre).reshape(count, cells, channels)

    over_columns(columns, cells, visit)


def forward_outer_kernel(z_ref, x_ref, low_ref, high_ref, weights_ref, slope_ref):
    columns, cells, channels = slope_ref.shape
    height = cells // 2
    top = x_ref.shape[1]

    def visit(k, count):
        parts = []
        for a in range(3):
            for b in range(3):
                near = pl.ds(k + b, count)
                if a == 0:
                    first = kept(z_ref[1], low_ref[near])
                else:
                    first = x_ref[near, (a - 1) * height : a * height]
                if a == 2:
                    last = kept(z_ref[2], high_ref[near])
                else:
                    last = x_ref[near, top - (2 - a) * height : top - (1 - a) * height]
                parts.append(jnp.concatenate([first, last], axis=1))
        pre = convolve(parts, weights_ref[...], channels, height, False)
        slope_ref[pl.ds(k, count)] = slope_of(pre).reshape(count, cells, channels)

    over_columns(columns, cells, visit)


def windows_kernel(z_ref, x_ref, low_ref, high_ref, out_ref):
    columns, _, cells = out_ref.shape[1:]
    height = low_ref.shape[1]

    def visit(k, count):
        for n in range(count):
            mid = x_ref[pl.ds(k + n + 1, 1)]
            low = kept(z_ref[1], low_ref[pl.ds(k + n + 1, 1)])
            high = kept(z_ref[2], high_ref[pl.ds(k + n + 1, 1)])
            out_ref[0, k + n] = window(mid, low, high, 0, height)[0].T
            out_ref[1, k + n] = window(mid, low, high, 2, height)[0].T

    over_columns(columns, cells, visit)


def grad_out_kernel(chan_count, height, z_ref, *refs):
    pieces = refs[:chan_count]
    inner_ref, outer_ref, grad_ref, bottom_ref, top_ref, hold_ref = refs[chan_count:]
    group = pieces[0].shape[1]
    columns, cells, _ = grad_ref.shape
    offsets = pair_offsets(z_ref[0], chan_count, group)

    def visit(k, count):
        for n in range(count):
            for j in range(chan_count):
                hold_ref[n, pl.ds(offsets[j], group), :] = pieces[j][k + n]
        for n in range(count):
            cot = hold_ref[n].T.astype(F32)
            outer = outer_ref[k + n]
            slope = jnp.concatenate([outer[:height], inner_ref[k + n], outer[height:]], axis=0)
            grad = (cot * slope).astype(BF16)
            grad_ref[k + n] = grad
            bottom_ref[k + n] = grad[:height]
            top_ref[k + n] = grad[cells - height :]

    over_columns(columns, cells, visit)


def filter_kernel(
    chan_count, space_count, shard, height, core_ref, x_ref, sides_ref, grad_ref, keep_ref, send_ref, acc_ref, pack_ref
):
    columns, cells, channels = grad_ref.shape
    group = channels // chan_count
    acc_ref[...] = jnp.zeros_like(acc_ref)

    def visit(k, count):
        lhs = jnp.concatenate(
            [
                jnp.concatenate(
                    [
                        x_ref[k + n + b + 1] if a == 1 else sides_ref[a // 2, k + n + b]
                        for n in range(count)
                    ],
                    axis=1,
                )
                for a in range(3)
                for b in range(3)
            ],
            axis=0,
        )
        grad = grad_ref[pl.ds(k + 1, count)].reshape(count * cells, channels).astype(F32)
        later, earlier = row_shifts(grad, height)
        rhs = jnp.concatenate([v.astype(BF16) for v in (later, grad, earlier)], axis=1)
        acc_ref[...] += jnp.dot(lhs, rhs, preferred_element_type=F32)

    over_columns(columns - 2, cells, visit)
    used = 27 * group
    for z in range(chan_count):
        for offset in range(27):
            a, t, m = offset // 9, offset // 3 % 3, offset % 3
            row = (3 * a + m) * channels + z * group
            pack_ref[z, offset * group : (offset + 1) * group, :] = acc_ref[
                row : row + group, t * channels : (t + 1) * channels
            ]
        pack_ref[z, used:, :] = jnp.zeros((space_count * shard - used, channels), F32)
    core = core_ref[0]
    for chip in range(space_count // 2):
        mine = pl.multiple_of((2 * chip + core) * shard, 8)
        other = pl.multiple_of((2 * chip + 1 - core) * shard, 8)
        for z in range(chan_count):
            keep_ref[chip, z] = pack_ref[z, pl.ds(mine, shard), :]
            send_ref[chip, z] = pack_ref[z, pl.ds(other, shard), :]


def input_kernel(chan_count, base, count, z_ref, grad_ref, low_ref, high_ref, weights_ref, *refs):
    made, outs, hold_ref = refs[: -1 - chan_count], refs[-1 - chan_count : -1], refs[-1]
    starts = [out.shape[0] - count for out in outs]
    for out, old in zip([out for out, start in zip(outs, starts) if start], made):
        out[: old.shape[0]] = old[...]
    columns, cells, channels = grad_ref.shape
    height = low_ref.shape[1]
    group = channels // chan_count
    offsets = group_offsets(z_ref[0], chan_count, group, 1)

    def visit(k, width):
        parts = [
            window(
                grad_ref[pl.ds(base + k + 2 - b, width)],
                kept(z_ref[1], low_ref[pl.ds(base + k + 2 - b, width)]),
                kept(z_ref[2], high_ref[pl.ds(base + k + 2 - b, width)]),
                2 - a,
                height,
            )
            for a in range(3)
            for b in range(3)
        ]
        total = convolve(parts, weights_ref[...], channels, height, True).astype(BF16)
        total = total.reshape(width, cells, channels)
        for n in range(width):
            hold_ref[n] = total[n].T
        for j in range(chan_count):
            for n in range(width):
                outs[j][starts[j] + k + n] = hold_ref[n, pl.ds(offsets[j], group), :]

    over_columns(count, cells, visit)


def call(kernel, outs, scratch, flops, args, scalar):
    nbytes = sum(math.prod(a.shape) * a.dtype.itemsize for a in list(args) + list(outs))
    return pl.pallas_call(
        kernel,
        out_shape=outs,
        in_specs=[pl.BlockSpec(memory_space=pltpu.SMEM)]
        + [pl.BlockSpec(memory_space=pltpu.VMEM)] * len(args),
        out_specs=[pl.BlockSpec(memory_space=pltpu.VMEM)] * len(outs),
        scratch_shapes=scratch,
        compiler_params=pltpu.CompilerParams(vmem_limit_bytes=VMEM_BYTES),
        cost_estimate=pl.CostEstimate(
            flops=flops, bytes_accessed=nbytes if flops else 0, transcendentals=0
        ),
    )(scalar, *args)


def column_blocks(array, before, behind, z, chan_count):
    group, planes, height, width = array.shape
    turned = array.reshape(group, planes * height, width).transpose(2, 0, 1)
    turned = jnp.pad(turned, ((before, behind), (0, 0), (0, 0)))
    columns = width // chan_count
    return [
        lax.dynamic_slice_in_dim(
            turned, (z ^ j) * columns, columns + before + behind, axis=0
        )
        for j in range(chan_count)
    ]


def swap(blocks):
    count = len(blocks)
    got = {
        j: lax.ppermute(blocks[j], "chan", [(i, i ^ j) for i in range(count)])
        for j in range(count - 1, 0, -1)
    }
    return [blocks[0]] + [got[j] for j in range(1, count)]


def exchange(blocks, axis):
    count = len(blocks)
    return [blocks[0]] + [
        lax.ppermute(blocks[j], axis, ring(count, j)) for j in range(1, count)
    ]


def fetch_filters(filters, s, chan_count, space_count):
    offsets, group, channels = filters.shape
    rows = offsets * group
    plan, sizes = share_plan(chan_count, space_count, rows)
    starts = [part * sizes[step] for step, part in plan]
    size = max(sizes)
    flat = jnp.pad(filters.reshape(rows, channels), ((0, max(starts) + size - rows), (0, 0)))
    far = chan_count - 1
    per_part = sum((s % far + 1 == k) * sizes[k] for k in range(1, chan_count))
    mine = lax.dynamic_slice_in_dim(flat, s // far * per_part, size, axis=0)
    route = [
        (place * chan_count + z, place * chan_count + (z + step) % chan_count)
        for place, (step, _) in enumerate(plan)
        for z in range(chan_count)
    ]
    return lax.ppermute(mine, ("space", "chan"), route)


def body(inputs, filters, cotangent):
    chan_count = lax.axis_size("chan")
    space_count = lax.axis_size("space")
    group, planes, height, width = inputs.shape
    channels = group * chan_count
    columns = width // chan_count
    cells = planes * height
    z = lax.axis_index("chan").astype(jnp.int32)
    s = lax.axis_index("space").astype(jnp.int32)
    upward, downward = ring(space_count, 1), ring(space_count, -1)
    shape = jax.ShapeDtypeStruct
    flags = [(s > 0).astype(jnp.int32), (s < space_count - 1).astype(jnp.int32)]
    z_arg = jnp.stack([z] + flags)
    macs = 27 * channels * channels * columns * cells

    share = fetch_filters(filters, s, chan_count, space_count)
    x_pieces = swap(after(column_blocks(inputs, 2, 2, z, chan_count), share))
    shares = lax.all_gather(share, "space", axis=0, tiled=False)
    c_blocks = column_blocks(after(cotangent, shares), 1, 4, z, chan_count)
    weights_f, weights_b = call(
        functools.partial(weights_kernel, chan_count),
        [shape((9 * channels, 3 * channels), BF16)] * 2,
        [],
        0,
        [filters, shares],
        z_arg,
    )
    x_pieces = after(x_pieces, weights_b, z_arg, c_blocks)

    x_first, x_cells, x_bottom, x_top = call(
        functools.partial(turn_kernel, chan_count, height),
        [
            shape((columns + 4, channels, cells), BF16),
            shape((columns + 4, cells, channels), BF16),
        ]
        + [shape((columns + 4, height, channels), BF16)] * 2,
        [],
        0,
        x_pieces,
        z_arg,
    )
    x_low = lax.ppermute(x_top, "space", upward)
    x_high = lax.ppermute(x_bottom, "space", downward)
    c_pieces = swap(c_blocks[:1] + [after(c, x) for c, x in zip(c_blocks[1:], x_pieces[1:])])
    slope_inner = call(
        functools.partial(forward_inner_kernel, height),
        [shape((columns + 2, cells - 2 * height, channels), F32)],
        [],
        0,
        [x_cells, weights_f],
        z_arg,
    )[0]
    slope_outer = call(
        forward_outer_kernel,
        [shape((columns + 2, 2 * height, channels), F32)],
        [],
        0,
        [after(x_cells, slope_inner), x_low, x_high, weights_f],
        z_arg,
    )[0]
    x_windows = call(
        windows_kernel,
        [shape((2, columns + 2, channels, cells), BF16)],
        [],
        0,
        [x_cells, x_low, x_high],
        z_arg,
    )[0]
    slope_outer = after(slope_outer, x_windows)
    grad, g_bottom, g_top = call(
        functools.partial(grad_out_kernel, chan_count, height),
        [shape((columns + 2, cells, channels), BF16)]
        + [shape((columns + 2, height, channels), BF16)] * 2,
        [pltpu.VMEM((block_step(cells), channels, cells), BF16)],
        10 * columns * cells * channels,
        [*c_pieces, slope_inner, slope_outer],
        z_arg,
    )
    g_low = lax.ppermute(g_top, "space", upward)
    g_high = lax.ppermute(g_bottom, "space", downward)

    chips = space_count // 2
    shard = -(-27 * group // (16 * space_count)) * 16
    half = shape((chips, chan_count, shard, channels), F32)
    keep, send = call(
        functools.partial(filter_kernel, chan_count, space_count, shard, height),
        [half, half],
        [
            pltpu.VMEM((9 * channels, 3 * channels), F32),
            pltpu.VMEM((chan_count, space_count * shard, channels), F32),
        ],
        0,
        [x_first, x_windows, grad],
        lax.rem(s, 2).reshape(1),
    )
    g_low, g_high, send = lax.optimization_barrier((g_low, g_high, send))
    from_core = lax.ppermute(send, "space", [(i, i ^ 1) for i in range(space_count)])
    early = columns // 2
    split = range(1, min(3, chan_count))
    hold = [pltpu.VMEM((block_step(cells), channels, cells), BF16)]
    first = call(
        functools.partial(input_kernel, chan_count, 0, early),
        [shape((early, group, cells), BF16)] * chan_count,
        hold,
        3 * macs,
        [grad, g_low, g_high, weights_b],
        z_arg,
    )
    returned_first = {j: lax.ppermute(first[j], "chan", ring(chan_count, j)) for j in split}
    pair_sum = keep + after(from_core, first[0])
    chip = s // 2
    chip_sum = lax.dynamic_index_in_dim(pair_sum, chip, 0, keepdims=False)
    rounded = pair_sum.astype(BF16)
    g_low, g_high = after((g_low, g_high), rounded)
    from_chips = []
    for k in range(1, chips):
        block = lax.dynamic_index_in_dim(rounded, chip ^ k, 0, keepdims=False)
        from_chips.append(
            lax.ppermute(block, "space", [(i, i ^ (2 * k)) for i in range(space_count)])
        )
    whole_blocks = [j for j in range(chan_count) if j not in split]
    back = call(
        functools.partial(input_kernel, chan_count, early, columns - early),
        [
            shape((columns if j in whole_blocks else columns - early, group, cells), BF16)
            for j in range(chan_count)
        ],
        hold,
        3 * macs,
        [grad, g_low, g_high, weights_b] + [first[j] for j in whole_blocks],
        z_arg,
    )
    from_chips, returned_first = after((from_chips, returned_first), back[0])
    for got in from_chips:
        chip_sum = chip_sum + got.astype(F32)
    chip_sum = after(chip_sum, returned_first)
    parts = [
        lax.dynamic_index_in_dim(chip_sum, lax.rem(z + j, chan_count), 0, keepdims=False)
        for j in range(chan_count)
    ]
    shard_sum = sum(exchange(parts, "chan"))
    returned = exchange(after(back, shard_sum), "chan")
    cell_total = planes * space_count * height * width
    shard_sum = shard_sum * (1.0 / math.sqrt(cell_total))
    whole = lax.all_gather(shard_sum, "space", axis=0, tiled=True)
    grad_w = whole[: 27 * group].reshape(27, group, channels)

    reverse = [
        part
        for j in range(chan_count)[::-1]
        for part in ([returned_first[j]] if j in split else []) + [returned[j]]
    ]
    doubled = jnp.concatenate(reverse + reverse, axis=0)
    start = lax.rem(chan_count - 1 - z + chan_count, chan_count) * columns
    ordered = lax.dynamic_slice_in_dim(doubled, start, width, axis=0)
    return ordered.transpose(1, 2, 0).reshape(group, planes, height, width), grad_w


def solution(mesh):
    placed = (P("chan", "space", None, None), P(None, "chan", None), P("chan", "space", None, None))
    return jax.shard_map(
        body,
        mesh=mesh,
        in_specs=placed,
        out_specs=(P("chan", "space", None, None), P(None, "chan", None)),
        check_vma=False,
    )
```

```python
import functools
import math

import jax
import jax.numpy as jnp
from jax import lax
from jax.experimental import pallas as pl
from jax.experimental.pallas import tpu as pltpu
from jax.sharding import PartitionSpec as P

BF16 = jnp.bfloat16
F32 = jnp.float32
VMEM_BYTES = 56 * 1024 * 1024


def ring(count, step):
    return [(i, (i + step) % count) for i in range(count)]


def after(value, *others):
    return lax.optimization_barrier((value, *others))[0]


def kept(flag, value):
    return jnp.where(flag > 0, value, jnp.zeros_like(value))


def window(mid, low, high, a, height):
    if a == 0:
        return jnp.concatenate([low, mid[:, :-height]], axis=1)
    if a == 2:
        return jnp.concatenate([mid[:, height:], high], axis=1)
    return mid


def row_shifts(value, height):
    split = value.reshape(-1, height, value.shape[-1])
    row = lax.broadcasted_iota(jnp.int32, split.shape, 1)
    later = jnp.where(row == height - 1, 0.0, pltpu.roll(split, height - 1, 1))
    earlier = jnp.where(row == 0, 0.0, pltpu.roll(split, 1, 1))
    return later.reshape(value.shape), earlier.reshape(value.shape)


def convolve(columns, weights, channels, height, mirrored):
    lhs = jnp.concatenate([c.reshape(-1, channels) for c in columns], axis=1)
    out = jnp.dot(lhs, weights, preferred_element_type=F32)
    first, mid, last = (out[:, t * channels : (t + 1) * channels] for t in range(3))
    if mirrored:
        first, last = last, first
    return mid + row_shifts(first, height)[1] + row_shifts(last, height)[0]


def group_offsets(z, chan_count, group, sign):
    return [
        pl.multiple_of(lax.rem(z + sign * j + chan_count, chan_count) * group, group)
        for j in range(chan_count)
    ]


def pair_offsets(z, chan_count, group):
    return [pl.multiple_of((z ^ j) * group, group) for j in range(chan_count)]


def block_step(rows):
    return max(1, 2048 // rows)


def over_columns(count, rows, visit):
    step = block_step(rows)
    loops, rest = count // step, count % step
    if loops:
        pl.loop(0, loops)(lambda i: visit(i * step, step))
    if rest:
        visit(loops * step, rest)


def turn_kernel(chan_count, height, z_ref, *refs):
    pieces = refs[:chan_count]
    first_ref, cells_ref, bottom_ref, top_ref = refs[chan_count:]
    columns, group, cells = pieces[0].shape
    offsets = pair_offsets(z_ref[0], chan_count, group)

    def visit(k, count):
        for n in range(count):
            for j in range(chan_count):
                first_ref[k + n, pl.ds(offsets[j], group), :] = pieces[j][k + n]
        for n in range(count):
            tile = first_ref[k + n].T
            cells_ref[k + n] = tile
            bottom_ref[k + n] = tile[:height]
            top_ref[k + n] = tile[cells - height :]

    over_columns(columns, cells, visit)


def share_plan(chan_count, space_count, rows):
    far = chan_count - 1
    plan = [(s % far + 1, s // far) for s in range(space_count)]
    counts = [0] + [sum(step == k for step, _ in plan) for k in range(1, chan_count)]
    return plan, [0] + [-(-rows // (16 * n)) * 16 for n in counts[1:]]


def weights_kernel(chan_count, z_ref, own_ref, shares_ref, forward_ref, backward_ref):
    offsets, group, channels = own_ref.shape
    plan, sizes = share_plan(chan_count, shares_ref.shape[0], offsets * group)
    places = group_offsets(z_ref[0], chan_count, group, -1)
    for offset in range(offsets):
        a, t, m = offset // 9, offset // 3 % 3, offset % 3
        for j in range(chan_count):
            for i in range(0, group, 16):
                if j == 0:
                    rows = own_ref[offset, i : i + 16]
                else:
                    source = offset * group + i
                    part, row = divmod(source, sizes[j])
                    rows = shares_ref[plan.index((j, part)), row : row + 16]
                row = pl.multiple_of((3 * a + m) * channels + places[j] + i, 16)
                forward_ref[pl.ds(row, 16), t * channels : (t + 1) * channels] = rows
    for k in range(9):
        for t in range(3):
            tile = (
                slice(k * channels, (k + 1) * channels),
                slice(t * channels, (t + 1) * channels),
            )
            backward_ref[tile] = forward_ref[tile].T


def slope_of(pre):
    sigma = 1.0 / (1.0 + jnp.exp(-pre))
    return sigma * (1.0 + pre * (1.0 - sigma))


def forward_inner_kernel(height, _, x_ref, weights_ref, slope_ref):
    columns, cells, channels = slope_ref.shape

    def visit(k, count):
        parts = [
            x_ref[pl.ds(k + b, count), a * height : a * height + cells]
            for a in range(3)
            for b in range(3)
        ]
        pre = convolve(parts, weights_ref[...], channels, height, False)
        slope_ref[pl.ds(k, count)] = slope_of(pre).reshape(count, cells, channels)

    over_columns(columns, cells, visit)


def forward_outer_kernel(z_ref, x_ref, low_ref, high_ref, weights_ref, slope_ref):
    columns, cells, channels = slope_ref.shape
    height = cells // 2
    top = x_ref.shape[1]

    def visit(k, count):
        parts = []
        for a in range(3):
            for b in range(3):
                near = pl.ds(k + b, count)
                if a == 0:
                    first = kept(z_ref[1], low_ref[near])
                else:
                    first = x_ref[near, (a - 1) * height : a * height]
                if a == 2:
                    last = kept(z_ref[2], high_ref[near])
                else:
                    last = x_ref[near, top - (2 - a) * height : top - (1 - a) * height]
                parts.append(jnp.concatenate([first, last], axis=1))
        pre = convolve(parts, weights_ref[...], channels, height, False)
        slope_ref[pl.ds(k, count)] = slope_of(pre).reshape(count, cells, channels)

    over_columns(columns, cells, visit)


def windows_kernel(z_ref, x_ref, low_ref, high_ref, out_ref):
    columns, _, cells = out_ref.shape[1:]
    height = low_ref.shape[1]

    def visit(k, count):
        for n in range(count):
            mid = x_ref[pl.ds(k + n + 1, 1)]
            low = kept(z_ref[1], low_ref[pl.ds(k + n + 1, 1)])
            high = kept(z_ref[2], high_ref[pl.ds(k + n + 1, 1)])
            out_ref[0, k + n] = window(mid, low, high, 0, height)[0].T
            out_ref[1, k + n] = window(mid, low, high, 2, height)[0].T

    over_columns(columns, cells, visit)


def grad_out_kernel(chan_count, height, z_ref, *refs):
    pieces = refs[:chan_count]
    inner_ref, outer_ref, grad_ref, bottom_ref, top_ref, hold_ref = refs[chan_count:]
    group = pieces[0].shape[1]
    columns, cells, _ = grad_ref.shape
    offsets = pair_offsets(z_ref[0], chan_count, group)

    def visit(k, count):
        for n in range(count):
            for j in range(chan_count):
                hold_ref[n, pl.ds(offsets[j], group), :] = pieces[j][k + n]
        for n in range(count):
            cot = hold_ref[n].T.astype(F32)
            outer = outer_ref[k + n]
            slope = jnp.concatenate([outer[:height], inner_ref[k + n], outer[height:]], axis=0)
            grad = (cot * slope).astype(BF16)
            grad_ref[k + n] = grad
            bottom_ref[k + n] = grad[:height]
            top_ref[k + n] = grad[cells - height :]

    over_columns(columns, cells, visit)


def filter_kernel(
    chan_count, space_count, shard, height, core_ref, x_ref, sides_ref, grad_ref, keep_ref, send_ref, acc_ref, pack_ref
):
    columns, cells, channels = grad_ref.shape
    group = channels // chan_count
    acc_ref[...] = jnp.zeros_like(acc_ref)

    def visit(k, count):
        lhs = jnp.concatenate(
            [
                jnp.concatenate(
                    [
                        x_ref[k + n + b + 1] if a == 1 else sides_ref[a // 2, k + n + b]
                        for n in range(count)
                    ],
                    axis=1,
                )
                for a in range(3)
                for b in range(3)
            ],
            axis=0,
        )
        grad = grad_ref[pl.ds(k + 1, count)].reshape(count * cells, channels).astype(F32)
        later, earlier = row_shifts(grad, height)
        rhs = jnp.concatenate([v.astype(BF16) for v in (later, grad, earlier)], axis=1)
        acc_ref[...] += jnp.dot(lhs, rhs, preferred_element_type=F32)

    over_columns(columns - 2, cells, visit)
    used = 27 * group
    for z in range(chan_count):
        for offset in range(27):
            a, t, m = offset // 9, offset // 3 % 3, offset % 3
            row = (3 * a + m) * channels + z * group
            pack_ref[z, offset * group : (offset + 1) * group, :] = acc_ref[
                row : row + group, t * channels : (t + 1) * channels
            ]
        pack_ref[z, used:, :] = jnp.zeros((space_count * shard - used, channels), F32)
    core = core_ref[0]
    for chip in range(space_count // 2):
        mine = pl.multiple_of((2 * chip + core) * shard, 8)
        other = pl.multiple_of((2 * chip + 1 - core) * shard, 8)
        for z in range(chan_count):
            keep_ref[chip, z] = pack_ref[z, pl.ds(mine, shard), :]
            send_ref[chip, z] = pack_ref[z, pl.ds(other, shard), :]


def input_kernel(chan_count, base, count, z_ref, grad_ref, low_ref, high_ref, weights_ref, *refs):
    made, outs, hold_ref = refs[: -1 - chan_count], refs[-1 - chan_count : -1], refs[-1]
    starts = [out.shape[0] - count for out in outs]
    for out, old in zip([out for out, start in zip(outs, starts) if start], made):
        out[: old.shape[0]] = old[...]
    columns, cells, channels = grad_ref.shape
    height = low_ref.shape[1]
    group = channels // chan_count
    offsets = group_offsets(z_ref[0], chan_count, group, 1)

    def visit(k, width):
        parts = [
            window(
                grad_ref[pl.ds(base + k + 2 - b, width)],
                kept(z_ref[1], low_ref[pl.ds(base + k + 2 - b, width)]),
                kept(z_ref[2], high_ref[pl.ds(base + k + 2 - b, width)]),
                2 - a,
                height,
            )
            for a in range(3)
            for b in range(3)
        ]
        total = convolve(parts, weights_ref[...], channels, height, True).astype(BF16)
        total = total.reshape(width, cells, channels)
        for n in range(width):
            hold_ref[n] = total[n].T
        for j in range(chan_count):
            for n in range(width):
                outs[j][starts[j] + k + n] = hold_ref[n, pl.ds(offsets[j], group), :]

    over_columns(count, cells, visit)


def call(kernel, outs, scratch, flops, args, scalar):
    nbytes = sum(math.prod(a.shape) * a.dtype.itemsize for a in list(args) + list(outs))
    return pl.pallas_call(
        kernel,
        out_shape=outs,
        in_specs=[pl.BlockSpec(memory_space=pltpu.SMEM)]
        + [pl.BlockSpec(memory_space=pltpu.VMEM)] * len(args),
        out_specs=[pl.BlockSpec(memory_space=pltpu.VMEM)] * len(outs),
        scratch_shapes=scratch,
        compiler_params=pltpu.CompilerParams(vmem_limit_bytes=VMEM_BYTES),
        cost_estimate=pl.CostEstimate(
            flops=flops, bytes_accessed=nbytes if flops else 0, transcendentals=0
        ),
    )(scalar, *args)


def column_blocks(array, before, behind, z, chan_count):
    group, planes, height, width = array.shape
    turned = array.reshape(group, planes * height, width).transpose(2, 0, 1)
    turned = jnp.pad(turned, ((before, behind), (0, 0), (0, 0)))
    columns = width // chan_count
    return [
        lax.dynamic_slice_in_dim(
            turned, (z ^ j) * columns, columns + before + behind, axis=0
        )
        for j in range(chan_count)
    ]


def swap(blocks):
    count = len(blocks)
    got = {
        j: lax.ppermute(blocks[j], "chan", [(i, i ^ j) for i in range(count)])
        for j in range(count - 1, 0, -1)
    }
    return [blocks[0]] + [got[j] for j in range(1, count)]


def exchange(blocks, axis):
    count = len(blocks)
    return [blocks[0]] + [
        lax.ppermute(blocks[j], axis, ring(count, j)) for j in range(1, count)
    ]


def fetch_filters(filters, s, chan_count, space_count):
    offsets, group, channels = filters.shape
    rows = offsets * group
    plan, sizes = share_plan(chan_count, space_count, rows)
    starts = [part * sizes[step] for step, part in plan]
    size = max(sizes)
    flat = jnp.pad(filters.reshape(rows, channels), ((0, max(starts) + size - rows), (0, 0)))
    far = chan_count - 1
    per_part = sum((s % far + 1 == k) * sizes[k] for k in range(1, chan_count))
    mine = lax.dynamic_slice_in_dim(flat, s // far * per_part, size, axis=0)
    route = [
        (place * chan_count + z, place * chan_count + (z + step) % chan_count)
        for place, (step, _) in enumerate(plan)
        for z in range(chan_count)
    ]
    return lax.ppermute(mine, ("space", "chan"), route)


def body(inputs, filters, cotangent):
    chan_count = lax.axis_size("chan")
    space_count = lax.axis_size("space")
    group, planes, height, width = inputs.shape
    channels = group * chan_count
    columns = width // chan_count
    cells = planes * height
    z = lax.axis_index("chan").astype(jnp.int32)
    s = lax.axis_index("space").astype(jnp.int32)
    upward, downward = ring(space_count, 1), ring(space_count, -1)
    shape = jax.ShapeDtypeStruct
    flags = [(s > 0).astype(jnp.int32), (s < space_count - 1).astype(jnp.int32)]
    z_arg = jnp.stack([z] + flags)
    macs = 27 * channels * channels * columns * cells

    share = fetch_filters(filters, s, chan_count, space_count)
    x_pieces = swap(after(column_blocks(inputs, 2, 2, z, chan_count), share))
    shares = lax.all_gather(share, "space", axis=0, tiled=False)
    c_blocks = column_blocks(after(cotangent, shares), 1, 4, z, chan_count)
    weights_f, weights_b = call(
        functools.partial(weights_kernel, chan_count),
        [shape((9 * channels, 3 * channels), BF16)] * 2,
        [],
        0,
        [filters, shares],
        z_arg,
    )
    gate, weights_b = after((x_pieces[2], weights_b), z_arg, c_blocks)
    x_pieces = after(x_pieces, weights_b)

    x_first, x_cells, x_bottom, x_top = call(
        functools.partial(turn_kernel, chan_count, height),
        [
            shape((columns + 4, channels, cells), BF16),
            shape((columns + 4, cells, channels), BF16),
        ]
        + [shape((columns + 4, height, channels), BF16)] * 2,
        [],
        0,
        x_pieces,
        z_arg,
    )
    x_low = lax.ppermute(x_top, "space", upward)
    x_high = lax.ppermute(x_bottom, "space", downward)
    c_pieces = swap(c_blocks[:1] + [after(c, gate) for c in c_blocks[1:]])
    slope_inner = call(
        functools.partial(forward_inner_kernel, height),
        [shape((columns + 2, cells - 2 * height, channels), F32)],
        [],
        0,
        [x_cells, weights_f],
        z_arg,
    )[0]
    slope_outer = call(
        forward_outer_kernel,
        [shape((columns + 2, 2 * height, channels), F32)],
        [],
        0,
        [after(x_cells, slope_inner), x_low, x_high, weights_f],
        z_arg,
    )[0]
    x_windows = call(
        windows_kernel,
        [shape((2, columns + 2, channels, cells), BF16)],
        [],
        0,
        [x_cells, x_low, x_high],
        z_arg,
    )[0]
    slope_outer = after(slope_outer, x_windows)
    grad, g_bottom, g_top = call(
        functools.partial(grad_out_kernel, chan_count, height),
        [shape((columns + 2, cells, channels), BF16)]
        + [shape((columns + 2, height, channels), BF16)] * 2,
        [pltpu.VMEM((block_step(cells), channels, cells), BF16)],
        10 * columns * cells * channels,
        [*c_pieces, slope_inner, slope_outer],
        z_arg,
    )
    g_low = lax.ppermute(g_top, "space", upward)
    g_high = lax.ppermute(g_bottom, "space", downward)

    chips = space_count // 2
    shard = -(-27 * group // (16 * space_count)) * 16
    half = shape((chips, chan_count, shard, channels), F32)
    keep, send = call(
        functools.partial(filter_kernel, chan_count, space_count, shard, height),
        [half, half],
        [
            pltpu.VMEM((9 * channels, 3 * channels), F32),
            pltpu.VMEM((chan_count, space_count * shard, channels), F32),
        ],
        0,
        [x_first, x_windows, grad],
        lax.rem(s, 2).reshape(1),
    )
    g_low, g_high, send = lax.optimization_barrier((g_low, g_high, send))
    from_core = lax.ppermute(send, "space", [(i, i ^ 1) for i in range(space_count)])
    early = columns // 2
    split = range(1, min(3, chan_count))
    hold = [pltpu.VMEM((block_step(cells), channels, cells), BF16)]
    first = call(
        functools.partial(input_kernel, chan_count, 0, early),
        [shape((early, group, cells), BF16)] * chan_count,
        hold,
        3 * macs,
        [grad, g_low, g_high, weights_b],
        z_arg,
    )
    returned_first = {j: lax.ppermute(first[j], "chan", ring(chan_count, j)) for j in split}
    pair_sum = keep + after(from_core, first[0])
    chip = s // 2
    chip_sum = lax.dynamic_index_in_dim(pair_sum, chip, 0, keepdims=False)
    rounded = pair_sum.astype(BF16)
    g_low, g_high = after((g_low, g_high), rounded)
    from_chips = []
    for k in range(1, chips):
        block = lax.dynamic_index_in_dim(rounded, chip ^ k, 0, keepdims=False)
        from_chips.append(
            lax.ppermute(block, "space", [(i, i ^ (2 * k)) for i in range(space_count)])
        )
    whole_blocks = [j for j in range(chan_count) if j not in split]
    back = call(
        functools.partial(input_kernel, chan_count, early, columns - early),
        [
            shape((columns if j in whole_blocks else columns - early, group, cells), BF16)
            for j in range(chan_count)
        ],
        hold,
        3 * macs,
        [grad, g_low, g_high, weights_b] + [first[j] for j in whole_blocks],
        z_arg,
    )
    from_chips, returned_first = after((from_chips, returned_first), back[0])
    for got in from_chips:
        chip_sum = chip_sum + got.astype(F32)
    chip_sum = after(chip_sum, returned_first)
    parts = [
        lax.dynamic_index_in_dim(chip_sum, lax.rem(z + j, chan_count), 0, keepdims=False)
        for j in range(chan_count)
    ]
    shard_sum = sum(exchange(parts, "chan"))
    returned = exchange(after(back, shard_sum), "chan")
    cell_total = planes * space_count * height * width
    shard_sum = shard_sum * (1.0 / math.sqrt(cell_total))
    whole = lax.all_gather(shard_sum, "space", axis=0, tiled=True)
    grad_w = whole[: 27 * group].reshape(27, group, channels)

    reverse = [
        part
        for j in range(chan_count)[::-1]
        for part in ([returned_first[j]] if j in split else []) + [returned[j]]
    ]
    doubled = jnp.concatenate(reverse + reverse, axis=0)
    start = lax.rem(chan_count - 1 - z + chan_count, chan_count) * columns
    ordered = lax.dynamic_slice_in_dim(doubled, start, width, axis=0)
    return ordered.transpose(1, 2, 0).reshape(group, planes, height, width), grad_w


def solution(mesh):
    placed = (P("chan", "space", None, None), P(None, "chan", None), P("chan", "space", None, None))
    return jax.shard_map(
        body,
        mesh=mesh,
        in_specs=placed,
        out_specs=(P("chan", "space", None, None), P(None, "chan", None)),
        check_vma=False,
    )
```

```python
import functools
import math

import jax
import jax.numpy as jnp
from jax import lax
from jax.experimental import pallas as pl
from jax.experimental.pallas import tpu as pltpu
from jax.sharding import PartitionSpec as P

BF16 = jnp.bfloat16
F32 = jnp.float32
VMEM_BYTES = 56 * 1024 * 1024


def ring(count, step):
    return [(i, (i + step) % count) for i in range(count)]


def after(value, *others):
    return lax.optimization_barrier((value, *others))[0]


def kept(flag, value):
    return jnp.where(flag > 0, value, jnp.zeros_like(value))


def window(mid, low, high, a, height):
    if a == 0:
        return jnp.concatenate([low, mid[:, :-height]], axis=1)
    if a == 2:
        return jnp.concatenate([mid[:, height:], high], axis=1)
    return mid


def row_shifts(value, height):
    split = value.reshape(-1, height, value.shape[-1])
    row = lax.broadcasted_iota(jnp.int32, split.shape, 1)
    later = jnp.where(row == height - 1, 0.0, pltpu.roll(split, height - 1, 1))
    earlier = jnp.where(row == 0, 0.0, pltpu.roll(split, 1, 1))
    return later.reshape(value.shape), earlier.reshape(value.shape)


def convolve(columns, weights, channels, height, mirrored):
    lhs = jnp.concatenate([c.reshape(-1, channels) for c in columns], axis=1)
    out = jnp.dot(lhs, weights, preferred_element_type=F32)
    first, mid, last = (out[:, t * channels : (t + 1) * channels] for t in range(3))
    if mirrored:
        first, last = last, first
    return mid + row_shifts(first, height)[1] + row_shifts(last, height)[0]


def group_offsets(z, chan_count, group, sign):
    return [
        pl.multiple_of(lax.rem(z + sign * j + chan_count, chan_count) * group, group)
        for j in range(chan_count)
    ]


def pair_offsets(z, chan_count, group):
    return [pl.multiple_of((z ^ j) * group, group) for j in range(chan_count)]


def block_step(rows):
    return max(1, 4096 // rows)


def over_columns(count, rows, visit):
    step = block_step(rows)
    loops, rest = count // step, count % step
    if loops:
        pl.loop(0, loops)(lambda i: visit(i * step, step))
    if rest:
        visit(loops * step, rest)


def turn_kernel(chan_count, height, z_ref, *refs):
    pieces = refs[:chan_count]
    first_ref, cells_ref, bottom_ref, top_ref = refs[chan_count:]
    columns, group, cells = pieces[0].shape
    offsets = pair_offsets(z_ref[0], chan_count, group)

    def visit(k, count):
        for n in range(count):
            for j in range(chan_count):
                first_ref[k + n, pl.ds(offsets[j], group), :] = pieces[j][k + n]
        for n in range(count):
            tile = first_ref[k + n].T
            cells_ref[k + n] = tile
            bottom_ref[k + n] = tile[:height]
            top_ref[k + n] = tile[cells - height :]

    over_columns(columns, cells, visit)


def share_plan(chan_count, space_count, rows):
    far = chan_count - 1
    plan = [(s % far + 1, s // far) for s in range(space_count)]
    counts = [0] + [sum(step == k for step, _ in plan) for k in range(1, chan_count)]
    return plan, [0] + [-(-rows // (16 * n)) * 16 for n in counts[1:]]


def weights_kernel(chan_count, z_ref, own_ref, shares_ref, forward_ref, backward_ref):
    offsets, group, channels = own_ref.shape
    plan, sizes = share_plan(chan_count, shares_ref.shape[0], offsets * group)
    places = group_offsets(z_ref[0], chan_count, group, -1)
    for offset in range(offsets):
        a, t, m = offset // 9, offset // 3 % 3, offset % 3
        for j in range(chan_count):
            for i in range(0, group, 16):
                if j == 0:
                    rows = own_ref[offset, i : i + 16]
                else:
                    source = offset * group + i
                    part, row = divmod(source, sizes[j])
                    rows = shares_ref[plan.index((j, part)), row : row + 16]
                row = pl.multiple_of((3 * a + m) * channels + places[j] + i, 16)
                forward_ref[pl.ds(row, 16), t * channels : (t + 1) * channels] = rows
    for k in range(9):
        for t in range(3):
            tile = (
                slice(k * channels, (k + 1) * channels),
                slice(t * channels, (t + 1) * channels),
            )
            backward_ref[tile] = forward_ref[tile].T


def slope_of(pre):
    sigma = 1.0 / (1.0 + jnp.exp(-pre))
    return sigma * (1.0 + pre * (1.0 - sigma))


def forward_inner_kernel(height, _, x_ref, weights_ref, slope_ref):
    columns, cells, channels = slope_ref.shape

    def visit(k, count):
        parts = [
            x_ref[pl.ds(k + b, count), a * height : a * height + cells]
            for a in range(3)
            for b in range(3)
        ]
        pre = convolve(parts, weights_ref[...], channels, height, False)
        slope_ref[pl.ds(k, count)] = slope_of(pre).reshape(count, cells, channels)

    over_columns(columns, cells, visit)


def forward_outer_kernel(z_ref, x_ref, low_ref, high_ref, weights_ref, slope_ref):
    columns, cells, channels = slope_ref.shape
    height = cells // 2
    top = x_ref.shape[1]

    def visit(k, count):
        parts = []
        for a in range(3):
            for b in range(3):
                near = pl.ds(k + b, count)
                if a == 0:
                    first = kept(z_ref[1], low_ref[near])
                else:
                    first = x_ref[near, (a - 1) * height : a * height]
                if a == 2:
                    last = kept(z_ref[2], high_ref[near])
                else:
                    last = x_ref[near, top - (2 - a) * height : top - (1 - a) * height]
                parts.append(jnp.concatenate([first, last], axis=1))
        pre = convolve(parts, weights_ref[...], channels, height, False)
        slope_ref[pl.ds(k, count)] = slope_of(pre).reshape(count, cells, channels)

    over_columns(columns, cells, visit)


def windows_kernel(z_ref, x_ref, low_ref, high_ref, out_ref):
    columns, _, cells = out_ref.shape[1:]
    height = low_ref.shape[1]

    def visit(k, count):
        for n in range(count):
            mid = x_ref[pl.ds(k + n + 1, 1)]
            low = kept(z_ref[1], low_ref[pl.ds(k + n + 1, 1)])
            high = kept(z_ref[2], high_ref[pl.ds(k + n + 1, 1)])
            out_ref[0, k + n] = window(mid, low, high, 0, height)[0].T
            out_ref[1, k + n] = window(mid, low, high, 2, height)[0].T

    over_columns(columns, cells, visit)


def grad_out_kernel(chan_count, height, z_ref, *refs):
    pieces = refs[:chan_count]
    inner_ref, outer_ref, grad_ref, bottom_ref, top_ref, hold_ref = refs[chan_count:]
    group = pieces[0].shape[1]
    columns, cells, _ = grad_ref.shape
    offsets = pair_offsets(z_ref[0], chan_count, group)

    def visit(k, count):
        for n in range(count):
            for j in range(chan_count):
                hold_ref[n, pl.ds(offsets[j], group), :] = pieces[j][k + n]
        for n in range(count):
            cot = hold_ref[n].T.astype(F32)
            outer = outer_ref[k + n]
            slope = jnp.concatenate([outer[:height], inner_ref[k + n], outer[height:]], axis=0)
            grad = (cot * slope).astype(BF16)
            grad_ref[k + n] = grad
            bottom_ref[k + n] = grad[:height]
            top_ref[k + n] = grad[cells - height :]

    over_columns(columns, cells, visit)


def filter_kernel(
    chan_count, space_count, shard, height, core_ref, x_ref, sides_ref, grad_ref, keep_ref, send_ref, acc_ref, pack_ref
):
    columns, cells, channels = grad_ref.shape
    group = channels // chan_count
    acc_ref[...] = jnp.zeros_like(acc_ref)

    def visit(k, count):
        lhs = jnp.concatenate(
            [
                jnp.concatenate(
                    [
                        x_ref[k + n + b + 1] if a == 1 else sides_ref[a // 2, k + n + b]
                        for n in range(count)
                    ],
                    axis=1,
                )
                for a in range(3)
                for b in range(3)
            ],
            axis=0,
        )
        grad = grad_ref[pl.ds(k + 1, count)].reshape(count * cells, channels).astype(F32)
        later, earlier = row_shifts(grad, height)
        rhs = jnp.concatenate([v.astype(BF16) for v in (later, grad, earlier)], axis=1)
        acc_ref[...] += jnp.dot(lhs, rhs, preferred_element_type=F32)

    over_columns(columns - 2, cells, visit)
    used = 27 * group
    for z in range(chan_count):
        for offset in range(27):
            a, t, m = offset // 9, offset // 3 % 3, offset % 3
            row = (3 * a + m) * channels + z * group
            pack_ref[z, offset * group : (offset + 1) * group, :] = acc_ref[
                row : row + group, t * channels : (t + 1) * channels
            ]
        pack_ref[z, used:, :] = jnp.zeros((space_count * shard - used, channels), F32)
    core = core_ref[0]
    for chip in range(space_count // 2):
        mine = pl.multiple_of((2 * chip + core) * shard, 8)
        other = pl.multiple_of((2 * chip + 1 - core) * shard, 8)
        for z in range(chan_count):
            keep_ref[chip, z] = pack_ref[z, pl.ds(mine, shard), :]
            send_ref[chip, z] = pack_ref[z, pl.ds(other, shard), :]


def input_kernel(chan_count, base, count, z_ref, grad_ref, low_ref, high_ref, weights_ref, *refs):
    made, outs, hold_ref = refs[: -1 - chan_count], refs[-1 - chan_count : -1], refs[-1]
    starts = [out.shape[0] - count for out in outs]
    for out, old in zip([out for out, start in zip(outs, starts) if start], made):
        out[: old.shape[0]] = old[...]
    columns, cells, channels = grad_ref.shape
    height = low_ref.shape[1]
    group = channels // chan_count
    offsets = group_offsets(z_ref[0], chan_count, group, 1)

    def visit(k, width):
        parts = [
            window(
                grad_ref[pl.ds(base + k + 2 - b, width)],
                kept(z_ref[1], low_ref[pl.ds(base + k + 2 - b, width)]),
                kept(z_ref[2], high_ref[pl.ds(base + k + 2 - b, width)]),
                2 - a,
                height,
            )
            for a in range(3)
            for b in range(3)
        ]
        total = convolve(parts, weights_ref[...], channels, height, True).astype(BF16)
        total = total.reshape(width, cells, channels)
        for n in range(width):
            hold_ref[n] = total[n].T
        for j in range(chan_count):
            for n in range(width):
                outs[j][starts[j] + k + n] = hold_ref[n, pl.ds(offsets[j], group), :]

    over_columns(count, cells, visit)


def call(kernel, outs, scratch, flops, args, scalar):
    nbytes = sum(math.prod(a.shape) * a.dtype.itemsize for a in list(args) + list(outs))
    return pl.pallas_call(
        kernel,
        out_shape=outs,
        in_specs=[pl.BlockSpec(memory_space=pltpu.SMEM)]
        + [pl.BlockSpec(memory_space=pltpu.VMEM)] * len(args),
        out_specs=[pl.BlockSpec(memory_space=pltpu.VMEM)] * len(outs),
        scratch_shapes=scratch,
        compiler_params=pltpu.CompilerParams(vmem_limit_bytes=VMEM_BYTES),
        cost_estimate=pl.CostEstimate(
            flops=flops, bytes_accessed=nbytes if flops else 0, transcendentals=0
        ),
    )(scalar, *args)


def column_blocks(array, before, behind, z, chan_count):
    group, planes, height, width = array.shape
    turned = array.reshape(group, planes * height, width).transpose(2, 0, 1)
    turned = jnp.pad(turned, ((before, behind), (0, 0), (0, 0)))
    columns = width // chan_count
    return [
        lax.dynamic_slice_in_dim(
            turned, (z ^ j) * columns, columns + before + behind, axis=0
        )
        for j in range(chan_count)
    ]


def swap(blocks):
    count = len(blocks)
    got = {
        j: lax.ppermute(blocks[j], "chan", [(i, i ^ j) for i in range(count)])
        for j in range(count - 1, 0, -1)
    }
    return [blocks[0]] + [got[j] for j in range(1, count)]


def exchange(blocks, axis):
    count = len(blocks)
    return [blocks[0]] + [
        lax.ppermute(blocks[j], axis, ring(count, j)) for j in range(1, count)
    ]


def fetch_filters(filters, s, chan_count, space_count):
    offsets, group, channels = filters.shape
    rows = offsets * group
    plan, sizes = share_plan(chan_count, space_count, rows)
    starts = [part * sizes[step] for step, part in plan]
    size = max(sizes)
    flat = jnp.pad(filters.reshape(rows, channels), ((0, max(starts) + size - rows), (0, 0)))
    far = chan_count - 1
    per_part = sum((s % far + 1 == k) * sizes[k] for k in range(1, chan_count))
    mine = lax.dynamic_slice_in_dim(flat, s // far * per_part, size, axis=0)
    route = [
        (place * chan_count + z, place * chan_count + (z + step) % chan_count)
        for place, (step, _) in enumerate(plan)
        for z in range(chan_count)
    ]
    return lax.ppermute(mine, ("space", "chan"), route)


def body(inputs, filters, cotangent):
    chan_count = lax.axis_size("chan")
    space_count = lax.axis_size("space")
    group, planes, height, width = inputs.shape
    channels = group * chan_count
    columns = width // chan_count
    cells = planes * height
    z = lax.axis_index("chan").astype(jnp.int32)
    s = lax.axis_index("space").astype(jnp.int32)
    upward, downward = ring(space_count, 1), ring(space_count, -1)
    shape = jax.ShapeDtypeStruct
    flags = [(s > 0).astype(jnp.int32), (s < space_count - 1).astype(jnp.int32)]
    z_arg = jnp.stack([z] + flags)
    macs = 27 * channels * channels * columns * cells

    share = fetch_filters(filters, s, chan_count, space_count)
    x_pieces = swap(after(column_blocks(inputs, 2, 2, z, chan_count), share))
    shares = lax.all_gather(share, "space", axis=0, tiled=False)
    c_blocks = column_blocks(after(cotangent, shares), 1, 4, z, chan_count)
    weights_f, weights_b = call(
        functools.partial(weights_kernel, chan_count),
        [shape((9 * channels, 3 * channels), BF16)] * 2,
        [],
        0,
        [filters, shares],
        z_arg,
    )
    gate, weights_b = after((x_pieces[2], weights_b), z_arg, c_blocks)
    x_pieces = after(x_pieces, weights_b)

    x_first, x_cells, x_bottom, x_top = call(
        functools.partial(turn_kernel, chan_count, height),
        [
            shape((columns + 4, channels, cells), BF16),
            shape((columns + 4, cells, channels), BF16),
        ]
        + [shape((columns + 4, height, channels), BF16)] * 2,
        [],
        0,
        x_pieces,
        z_arg,
    )
    x_low = lax.ppermute(x_top, "space", upward)
    x_high = lax.ppermute(x_bottom, "space", downward)
    c_pieces = swap(c_blocks[:1] + [after(c, gate) for c in c_blocks[1:]])
    slope_inner = call(
        functools.partial(forward_inner_kernel, height),
        [shape((columns + 2, cells - 2 * height, channels), F32)],
        [],
        0,
        [x_cells, weights_f],
        z_arg,
    )[0]
    slope_outer = call(
        forward_outer_kernel,
        [shape((columns + 2, 2 * height, channels), F32)],
        [],
        0,
        [after(x_cells, slope_inner), x_low, x_high, weights_f],
        z_arg,
    )[0]
    x_windows = call(
        windows_kernel,
        [shape((2, columns + 2, channels, cells), BF16)],
        [],
        0,
        [x_cells, x_low, x_high],
        z_arg,
    )[0]
    slope_outer = after(slope_outer, x_windows)
    grad, g_bottom, g_top = call(
        functools.partial(grad_out_kernel, chan_count, height),
        [shape((columns + 2, cells, channels), BF16)]
        + [shape((columns + 2, height, channels), BF16)] * 2,
        [pltpu.VMEM((block_step(cells), channels, cells), BF16)],
        10 * columns * cells * channels,
        [*c_pieces, slope_inner, slope_outer],
        z_arg,
    )
    g_low = lax.ppermute(g_top, "space", upward)
    g_high = lax.ppermute(g_bottom, "space", downward)

    chips = space_count // 2
    shard = -(-27 * group // (16 * space_count)) * 16
    half = shape((chips, chan_count, shard, channels), F32)
    keep, send = call(
        functools.partial(filter_kernel, chan_count, space_count, shard, height),
        [half, half],
        [
            pltpu.VMEM((9 * channels, 3 * channels), F32),
            pltpu.VMEM((chan_count, space_count * shard, channels), F32),
        ],
        0,
        [x_first, x_windows, grad],
        lax.rem(s, 2).reshape(1),
    )
    g_low, g_high, send = lax.optimization_barrier((g_low, g_high, send))
    from_core = lax.ppermute(send, "space", [(i, i ^ 1) for i in range(space_count)])
    early = columns // 2
    split = range(1, min(3, chan_count))
    hold = [pltpu.VMEM((block_step(cells), channels, cells), BF16)]
    first = call(
        functools.partial(input_kernel, chan_count, 0, early),
        [shape((early, group, cells), BF16)] * chan_count,
        hold,
        3 * macs,
        [grad, g_low, g_high, weights_b],
        z_arg,
    )
    returned_first = {j: lax.ppermute(first[j], "chan", ring(chan_count, j)) for j in split}
    pair_sum = keep + after(from_core, first[0])
    chip = s // 2
    chip_sum = lax.dynamic_index_in_dim(pair_sum, chip, 0, keepdims=False)
    rounded = pair_sum.astype(BF16)
    g_low, g_high = after((g_low, g_high), rounded)
    from_chips = []
    for k in range(1, chips):
        block = lax.dynamic_index_in_dim(rounded, chip ^ k, 0, keepdims=False)
        from_chips.append(
            lax.ppermute(block, "space", [(i, i ^ (2 * k)) for i in range(space_count)])
        )
    whole_blocks = [j for j in range(chan_count) if j not in split]
    back = call(
        functools.partial(input_kernel, chan_count, early, columns - early),
        [
            shape((columns if j in whole_blocks else columns - early, group, cells), BF16)
            for j in range(chan_count)
        ],
        hold,
        3 * macs,
        [grad, g_low, g_high, weights_b] + [first[j] for j in whole_blocks],
        z_arg,
    )
    from_chips, returned_first = after((from_chips, returned_first), back[0])
    for got in from_chips:
        chip_sum = chip_sum + got.astype(F32)
    chip_sum = after(chip_sum, returned_first)
    parts = [
        lax.dynamic_index_in_dim(chip_sum, lax.rem(z + j, chan_count), 0, keepdims=False)
        for j in range(chan_count)
    ]
    summed = exchange(parts, "chan")
    shard_sum = sum(summed)
    returned = exchange(after(back, summed[2]), "chan")
    cell_total = planes * space_count * height * width
    shard_sum = shard_sum * (1.0 / math.sqrt(cell_total))
    whole = lax.all_gather(shard_sum, "space", axis=0, tiled=True)
    grad_w = whole[: 27 * group].reshape(27, group, channels)

    reverse = [
        part
        for j in range(chan_count)[::-1]
        for part in ([returned_first[j]] if j in split else []) + [returned[j]]
    ]
    doubled = jnp.concatenate(reverse + reverse, axis=0)
    start = lax.rem(chan_count - 1 - z + chan_count, chan_count) * columns
    ordered = lax.dynamic_slice_in_dim(doubled, start, width, axis=0)
    return ordered.transpose(1, 2, 0).reshape(group, planes, height, width), grad_w


def solution(mesh):
    placed = (P("chan", "space", None, None), P(None, "chan", None), P("chan", "space", None, None))
    return jax.shard_map(
        body,
        mesh=mesh,
        in_specs=placed,
        out_specs=(P("chan", "space", None, None), P(None, "chan", None)),
        check_vma=False,
    )
```

```python
import functools
import math

import jax
import jax.numpy as jnp
from jax import lax
from jax.experimental import pallas as pl
from jax.experimental.pallas import tpu as pltpu
from jax.sharding import PartitionSpec as P

BF16 = jnp.bfloat16
F32 = jnp.float32
VMEM_BYTES = 56 * 1024 * 1024


def ring(count, step):
    return [(i, (i + step) % count) for i in range(count)]


def after(value, *others):
    return lax.optimization_barrier((value, *others))[0]


def kept(flag, value):
    return jnp.where(flag > 0, value, jnp.zeros_like(value))


def window(mid, low, high, a, height):
    if a == 0:
        return jnp.concatenate([low, mid[:, :-height]], axis=1)
    if a == 2:
        return jnp.concatenate([mid[:, height:], high], axis=1)
    return mid


def row_shifts(value, height):
    split = value.reshape(-1, height, value.shape[-1])
    row = lax.broadcasted_iota(jnp.int32, split.shape, 1)
    later = jnp.where(row == height - 1, 0.0, pltpu.roll(split, height - 1, 1))
    earlier = jnp.where(row == 0, 0.0, pltpu.roll(split, 1, 1))
    return later.reshape(value.shape), earlier.reshape(value.shape)


def convolve(columns, weights, channels, height, mirrored):
    lhs = jnp.concatenate([c.reshape(-1, channels) for c in columns], axis=1)
    out = jnp.dot(lhs, weights, preferred_element_type=F32)
    first, mid, last = (out[:, t * channels : (t + 1) * channels] for t in range(3))
    if mirrored:
        first, last = last, first
    return mid + row_shifts(first, height)[1] + row_shifts(last, height)[0]


def group_offsets(z, chan_count, group, sign):
    return [
        pl.multiple_of(lax.rem(z + sign * j + chan_count, chan_count) * group, group)
        for j in range(chan_count)
    ]


def pair_offsets(z, chan_count, group):
    return [pl.multiple_of((z ^ j) * group, group) for j in range(chan_count)]


def block_step(rows):
    return max(1, 4096 // rows)


def over_columns(count, rows, visit):
    step = block_step(rows)
    loops, rest = count // step, count % step
    if loops == 1:
        visit(0, step)
    elif loops:
        pl.loop(0, loops)(lambda i: visit(i * step, step))
    if rest:
        visit(loops * step, rest)


def turn_kernel(chan_count, height, z_ref, *refs):
    pieces = refs[:chan_count]
    first_ref, cells_ref, bottom_ref, top_ref = refs[chan_count:]
    columns, group, cells = pieces[0].shape
    offsets = pair_offsets(z_ref[0], chan_count, group)

    def visit(k, count):
        for n in range(count):
            for j in range(chan_count):
                first_ref[k + n, pl.ds(offsets[j], group), :] = pieces[j][k + n]
        for n in range(count):
            tile = first_ref[k + n].T
            cells_ref[k + n] = tile
            bottom_ref[k + n] = tile[:height]
            top_ref[k + n] = tile[cells - height :]

    over_columns(columns, cells, visit)


def share_plan(chan_count, space_count, rows):
    far = chan_count - 1
    plan = [(s % far + 1, s // far) for s in range(space_count)]
    counts = [0] + [sum(step == k for step, _ in plan) for k in range(1, chan_count)]
    return plan, [0] + [-(-rows // (16 * n)) * 16 for n in counts[1:]]


def weights_kernel(chan_count, z_ref, own_ref, shares_ref, forward_ref, backward_ref):
    offsets, group, channels = own_ref.shape
    plan, sizes = share_plan(chan_count, shares_ref.shape[0], offsets * group)
    places = group_offsets(z_ref[0], chan_count, group, -1)
    for offset in range(offsets):
        a, t, m = offset // 9, offset // 3 % 3, offset % 3
        for j in range(chan_count):
            for i in range(0, group, 16):
                if j == 0:
                    rows = own_ref[offset, i : i + 16]
                else:
                    source = offset * group + i
                    part, row = divmod(source, sizes[j])
                    rows = shares_ref[plan.index((j, part)), row : row + 16]
                row = pl.multiple_of((3 * a + m) * channels + places[j] + i, 16)
                forward_ref[pl.ds(row, 16), t * channels : (t + 1) * channels] = rows
    for k in range(9):
        for t in range(3):
            tile = (
                slice(k * channels, (k + 1) * channels),
                slice(t * channels, (t + 1) * channels),
            )
            backward_ref[tile] = forward_ref[tile].T


def slope_of(pre):
    sigma = 1.0 / (1.0 + jnp.exp(-pre))
    return sigma * (1.0 + pre * (1.0 - sigma))


def forward_inner_kernel(height, _, x_ref, weights_ref, slope_ref):
    columns, cells, channels = slope_ref.shape

    def visit(k, count):
        parts = [
            x_ref[pl.ds(k + b, count), a * height : a * height + cells]
            for a in range(3)
            for b in range(3)
        ]
        pre = convolve(parts, weights_ref[...], channels, height, False)
        slope_ref[pl.ds(k, count)] = slope_of(pre).reshape(count, cells, channels)

    over_columns(columns, cells, visit)


def forward_outer_kernel(z_ref, x_ref, low_ref, high_ref, weights_ref, slope_ref):
    columns, cells, channels = slope_ref.shape
    height = cells // 2
    top = x_ref.shape[1]

    def visit(k, count):
        parts = []
        for a in range(3):
            for b in range(3):
                near = pl.ds(k + b, count)
                if a == 0:
                    first = kept(z_ref[1], low_ref[near])
                else:
                    first = x_ref[near, (a - 1) * height : a * height]
                if a == 2:
                    last = kept(z_ref[2], high_ref[near])
                else:
                    last = x_ref[near, top - (2 - a) * height : top - (1 - a) * height]
                parts.append(jnp.concatenate([first, last], axis=1))
        pre = convolve(parts, weights_ref[...], channels, height, False)
        slope_ref[pl.ds(k, count)] = slope_of(pre).reshape(count, cells, channels)

    over_columns(columns, cells, visit)


def windows_kernel(z_ref, x_ref, low_ref, high_ref, out_ref):
    columns, _, cells = out_ref.shape[1:]
    height = low_ref.shape[1]

    def visit(k, count):
        for n in range(count):
            mid = x_ref[pl.ds(k + n + 1, 1)]
            low = kept(z_ref[1], low_ref[pl.ds(k + n + 1, 1)])
            high = kept(z_ref[2], high_ref[pl.ds(k + n + 1, 1)])
            out_ref[0, k + n] = window(mid, low, high, 0, height)[0].T
            out_ref[1, k + n] = window(mid, low, high, 2, height)[0].T

    over_columns(columns, cells, visit)


def grad_out_kernel(chan_count, height, z_ref, *refs):
    pieces = refs[:chan_count]
    inner_ref, outer_ref, grad_ref, bottom_ref, top_ref, hold_ref = refs[chan_count:]
    group = pieces[0].shape[1]
    columns, cells, _ = grad_ref.shape
    offsets = pair_offsets(z_ref[0], chan_count, group)

    def visit(k, count):
        for n in range(count):
            for j in range(chan_count):
                hold_ref[n, pl.ds(offsets[j], group), :] = pieces[j][k + n]
        for n in range(count):
            cot = hold_ref[n].T.astype(F32)
            outer = outer_ref[k + n]
            slope = jnp.concatenate([outer[:height], inner_ref[k + n], outer[height:]], axis=0)
            grad = (cot * slope).astype(BF16)
            grad_ref[k + n] = grad
            bottom_ref[k + n] = grad[:height]
            top_ref[k + n] = grad[cells - height :]

    over_columns(columns, cells, visit)


def filter_kernel(
    chan_count, space_count, shard, height, core_ref, x_ref, sides_ref, grad_ref, keep_ref, send_ref, acc_ref, pack_ref
):
    columns, cells, channels = grad_ref.shape
    group = channels // chan_count
    single = columns - 2 <= block_step(cells)
    if not single:
        acc_ref[...] = jnp.zeros_like(acc_ref)

    def visit(k, count):
        lhs = jnp.concatenate(
            [
                jnp.concatenate(
                    [
                        x_ref[k + n + b + 1] if a == 1 else sides_ref[a // 2, k + n + b]
                        for n in range(count)
                    ],
                    axis=1,
                )
                for a in range(3)
                for b in range(3)
            ],
            axis=0,
        )
        grad = grad_ref[pl.ds(k + 1, count)].reshape(count * cells, channels).astype(F32)
        later, earlier = row_shifts(grad, height)
        rhs = jnp.concatenate([v.astype(BF16) for v in (later, grad, earlier)], axis=1)
        product = jnp.dot(lhs, rhs, preferred_element_type=F32)
        acc_ref[...] = product if single else acc_ref[...] + product

    over_columns(columns - 2, cells, visit)
    used = 27 * group
    for z in range(chan_count):
        for offset in range(27):
            a, t, m = offset // 9, offset // 3 % 3, offset % 3
            row = (3 * a + m) * channels + z * group
            pack_ref[z, offset * group : (offset + 1) * group, :] = acc_ref[
                row : row + group, t * channels : (t + 1) * channels
            ]
        pack_ref[z, used:, :] = jnp.zeros((space_count * shard - used, channels), F32)
    core = core_ref[0]
    for chip in range(space_count // 2):
        mine = pl.multiple_of((2 * chip + core) * shard, 8)
        other = pl.multiple_of((2 * chip + 1 - core) * shard, 8)
        for z in range(chan_count):
            keep_ref[chip, z] = pack_ref[z, pl.ds(mine, shard), :]
            send_ref[chip, z] = pack_ref[z, pl.ds(other, shard), :]


def input_kernel(chan_count, base, count, z_ref, grad_ref, low_ref, high_ref, weights_ref, *refs):
    made, outs, hold_ref = refs[: -1 - chan_count], refs[-1 - chan_count : -1], refs[-1]
    starts = [out.shape[0] - count for out in outs]
    for out, old in zip([out for out, start in zip(outs, starts) if start], made):
        out[: old.shape[0]] = old[...]
    columns, cells, channels = grad_ref.shape
    height = low_ref.shape[1]
    group = channels // chan_count
    offsets = group_offsets(z_ref[0], chan_count, group, 1)

    def visit(k, width):
        parts = [
            window(
                grad_ref[pl.ds(base + k + 2 - b, width)],
                kept(z_ref[1], low_ref[pl.ds(base + k + 2 - b, width)]),
                kept(z_ref[2], high_ref[pl.ds(base + k + 2 - b, width)]),
                2 - a,
                height,
            )
            for a in range(3)
            for b in range(3)
        ]
        total = convolve(parts, weights_ref[...], channels, height, True).astype(BF16)
        total = total.reshape(width, cells, channels)
        for n in range(width):
            hold_ref[n] = total[n].T
        for j in range(chan_count):
            for n in range(width):
                outs[j][starts[j] + k + n] = hold_ref[n, pl.ds(offsets[j], group), :]

    over_columns(count, cells, visit)


def call(kernel, outs, scratch, flops, args, scalar):
    nbytes = sum(math.prod(a.shape) * a.dtype.itemsize for a in list(args) + list(outs))
    return pl.pallas_call(
        kernel,
        out_shape=outs,
        in_specs=[pl.BlockSpec(memory_space=pltpu.SMEM)]
        + [pl.BlockSpec(memory_space=pltpu.VMEM)] * len(args),
        out_specs=[pl.BlockSpec(memory_space=pltpu.VMEM)] * len(outs),
        scratch_shapes=scratch,
        compiler_params=pltpu.CompilerParams(vmem_limit_bytes=VMEM_BYTES),
        cost_estimate=pl.CostEstimate(
            flops=flops, bytes_accessed=nbytes if flops else 0, transcendentals=0
        ),
    )(scalar, *args)


def column_blocks(array, before, behind, z, chan_count):
    group, planes, height, width = array.shape
    turned = array.reshape(group, planes * height, width).transpose(2, 0, 1)
    turned = jnp.pad(turned, ((before, behind), (0, 0), (0, 0)))
    columns = width // chan_count
    return [
        lax.dynamic_slice_in_dim(
            turned, (z ^ j) * columns, columns + before + behind, axis=0
        )
        for j in range(chan_count)
    ]


def swap(blocks):
    count = len(blocks)
    got = {
        j: lax.ppermute(blocks[j], "chan", [(i, i ^ j) for i in range(count)])
        for j in range(count - 1, 0, -1)
    }
    return [blocks[0]] + [got[j] for j in range(1, count)]


def exchange(blocks, axis):
    count = len(blocks)
    return [blocks[0]] + [
        lax.ppermute(blocks[j], axis, ring(count, j)) for j in range(1, count)
    ]


def fetch_filters(filters, s, chan_count, space_count):
    offsets, group, channels = filters.shape
    rows = offsets * group
    plan, sizes = share_plan(chan_count, space_count, rows)
    starts = [part * sizes[step] for step, part in plan]
    size = max(sizes)
    flat = jnp.pad(filters.reshape(rows, channels), ((0, max(starts) + size - rows), (0, 0)))
    far = chan_count - 1
    per_part = sum((s % far + 1 == k) * sizes[k] for k in range(1, chan_count))
    mine = lax.dynamic_slice_in_dim(flat, s // far * per_part, size, axis=0)
    route = [
        (place * chan_count + z, place * chan_count + (z + step) % chan_count)
        for place, (step, _) in enumerate(plan)
        for z in range(chan_count)
    ]
    return lax.ppermute(mine, ("space", "chan"), route)


def body(inputs, filters, cotangent):
    chan_count = lax.axis_size("chan")
    space_count = lax.axis_size("space")
    group, planes, height, width = inputs.shape
    channels = group * chan_count
    columns = width // chan_count
    cells = planes * height
    z = lax.axis_index("chan").astype(jnp.int32)
    s = lax.axis_index("space").astype(jnp.int32)
    upward, downward = ring(space_count, 1), ring(space_count, -1)
    shape = jax.ShapeDtypeStruct
    flags = [(s > 0).astype(jnp.int32), (s < space_count - 1).astype(jnp.int32)]
    z_arg = jnp.stack([z] + flags)
    macs = 27 * channels * channels * columns * cells

    share = fetch_filters(filters, s, chan_count, space_count)
    x_pieces = swap(after(column_blocks(inputs, 2, 2, z, chan_count), share))
    shares = lax.all_gather(share, "space", axis=0, tiled=False)
    c_blocks = column_blocks(after(cotangent, shares), 1, 4, z, chan_count)
    weights_f, weights_b = call(
        functools.partial(weights_kernel, chan_count),
        [shape((9 * channels, 3 * channels), BF16)] * 2,
        [],
        0,
        [filters, shares],
        z_arg,
    )
    gate, weights_b = after((x_pieces[2], weights_b), z_arg, c_blocks)
    x_pieces = after(x_pieces, weights_b)

    x_first, x_cells, x_bottom, x_top = call(
        functools.partial(turn_kernel, chan_count, height),
        [
            shape((columns + 4, channels, cells), BF16),
            shape((columns + 4, cells, channels), BF16),
        ]
        + [shape((columns + 4, height, channels), BF16)] * 2,
        [],
        0,
        x_pieces,
        z_arg,
    )
    x_low = lax.ppermute(x_top, "space", upward)
    x_high = lax.ppermute(x_bottom, "space", downward)
    c_pieces = swap(c_blocks[:1] + [after(c, gate) for c in c_blocks[1:]])
    slope_inner = call(
        functools.partial(forward_inner_kernel, height),
        [shape((columns + 2, cells - 2 * height, channels), F32)],
        [],
        0,
        [x_cells, weights_f],
        z_arg,
    )[0]
    slope_outer = call(
        forward_outer_kernel,
        [shape((columns + 2, 2 * height, channels), F32)],
        [],
        0,
        [after(x_cells, slope_inner), x_low, x_high, weights_f],
        z_arg,
    )[0]
    x_windows = call(
        windows_kernel,
        [shape((2, columns + 2, channels, cells), BF16)],
        [],
        0,
        [x_cells, x_low, x_high],
        z_arg,
    )[0]
    slope_outer = after(slope_outer, x_windows)
    grad, g_bottom, g_top = call(
        functools.partial(grad_out_kernel, chan_count, height),
        [shape((columns + 2, cells, channels), BF16)]
        + [shape((columns + 2, height, channels), BF16)] * 2,
        [pltpu.VMEM((block_step(cells), channels, cells), BF16)],
        10 * columns * cells * channels,
        [*c_pieces, slope_inner, slope_outer],
        z_arg,
    )
    g_low = lax.ppermute(g_top, "space", upward)
    g_high = lax.ppermute(g_bottom, "space", downward)

    chips = space_count // 2
    shard = -(-27 * group // (16 * space_count)) * 16
    half = shape((chips, chan_count, shard, channels), F32)
    keep, send = call(
        functools.partial(filter_kernel, chan_count, space_count, shard, height),
        [half, half],
        [
            pltpu.VMEM((9 * channels, 3 * channels), F32),
            pltpu.VMEM((chan_count, space_count * shard, channels), F32),
        ],
        0,
        [x_first, x_windows, grad],
        lax.rem(s, 2).reshape(1),
    )
    g_low, g_high, send = lax.optimization_barrier((g_low, g_high, send))
    from_core = lax.ppermute(send, "space", [(i, i ^ 1) for i in range(space_count)])
    early = columns // 2
    split = range(1, min(3, chan_count))
    hold = [pltpu.VMEM((block_step(cells), channels, cells), BF16)]
    first = call(
        functools.partial(input_kernel, chan_count, 0, early),
        [shape((early, group, cells), BF16)] * chan_count,
        hold,
        3 * macs,
        [grad, g_low, g_high, weights_b],
        z_arg,
    )
    returned_first = {j: lax.ppermute(first[j], "chan", ring(chan_count, j)) for j in split}
    pair_sum = keep + after(from_core, first[0])
    chip = s // 2
    chip_sum = lax.dynamic_index_in_dim(pair_sum, chip, 0, keepdims=False)
    rounded = pair_sum.astype(BF16)
    g_low, g_high = after((g_low, g_high), rounded)
    from_chips = []
    for k in range(1, chips):
        block = lax.dynamic_index_in_dim(rounded, chip ^ k, 0, keepdims=False)
        from_chips.append(
            lax.ppermute(block, "space", [(i, i ^ (2 * k)) for i in range(space_count)])
        )
    whole_blocks = [j for j in range(chan_count) if j not in split]
    back = call(
        functools.partial(input_kernel, chan_count, early, columns - early),
        [
            shape((columns if j in whole_blocks else columns - early, group, cells), BF16)
            for j in range(chan_count)
        ],
        hold,
        3 * macs,
        [grad, g_low, g_high, weights_b] + [first[j] for j in whole_blocks],
        z_arg,
    )
    from_chips, returned_first = after((from_chips, returned_first), back[0])
    for got in from_chips:
        chip_sum = chip_sum + got.astype(F32)
    chip_sum = after(chip_sum, returned_first)
    parts = [
        lax.dynamic_index_in_dim(chip_sum, lax.rem(z + j, chan_count), 0, keepdims=False)
        for j in range(chan_count)
    ]
    summed = exchange(parts, "chan")
    shard_sum = sum(summed)
    gated = [after(block, shard_sum if j in split else summed[2]) for j, block in enumerate(back)]
    returned = exchange(gated, "chan")
    cell_total = planes * space_count * height * width
    shard_sum = shard_sum * (1.0 / math.sqrt(cell_total))
    whole = lax.all_gather(shard_sum, "space", axis=0, tiled=True)
    grad_w = whole[: 27 * group].reshape(27, group, channels)

    reverse = [
        part
        for j in range(chan_count)[::-1]
        for part in ([returned_first[j]] if j in split else []) + [returned[j]]
    ]
    doubled = jnp.concatenate(reverse + reverse, axis=0)
    start = lax.rem(chan_count - 1 - z + chan_count, chan_count) * columns
    ordered = lax.dynamic_slice_in_dim(doubled, start, width, axis=0)
    return ordered.transpose(1, 2, 0).reshape(group, planes, height, width), grad_w


def solution(mesh):
    placed = (P("chan", "space", None, None), P(None, "chan", None), P("chan", "space", None, None))
    return jax.shard_map(
        body,
        mesh=mesh,
        in_specs=placed,
        out_specs=(P("chan", "space", None, None), P(None, "chan", None)),
        check_vma=False,
    )
```
